256 devices in a mesh: dp: 64 (over y, z, core), shard: 4 (over x).
Axes of the slice: x: 4, y: 4, z: 8, core: 2. Of those that a mesh axis runs over, the one named last changes fastest.
Arguments:
- waveform: bfloat16 [512, 6400], P(('dp', 'shard')), may hold values from -6 to 6
- lengths: int32 [512], P(('dp', 'shard')), may hold values from 1600 to 6400
- source: int32 [512], P(('dp', 'shard')), may hold values from 0 to 511, as said below
- frame_mask: int32 [512, 639], P(('dp', 'shard')), may hold values 0 or 1
- cotangent: bfloat16 [512, 639, 512], P(('dp', 'shard')), may hold values from -6 to 6
- conv1_weight: bfloat16 [10, 512], replicated, may hold values from -2 to 2
- gain_one: float32 [512], replicated, may hold values from 0.5 to 2
- shift_one: float32 [512], replicated, may hold values from -3 to 3
- conv2_weight: bfloat16 [1536, 512], P('shard'), may hold values from -0.15625 to 0.15625
- gain_two: float32 [512], replicated, may hold values from 0.5 to 2
- shift_two: float32 [512], replicated, may hold values from -3 to 3
Outputs:
- features: bfloat16 [512, 639, 512], P(('dp', 'shard'))
- grad_conv2: float32 [1536, 512], P('shard')
- grad_front: float32 [14, 512], replicated
The draws below stay inside these ranges and needn't reach their ends.
Inputs may be any that keep to these rules, and one draw needn't show every extreme that they name: `source`: a permutation of the crops; the crop placed at slot g was loaded on a device with the same index along shard as the device of slot g.
All inputs are finite; a program needn't handle non-finite values. No bound on the sum of `frame_mask` on one device may be relied on, other than what follows from the above.
Results may differ from the reference program's by a relative error of at most 0.006.
Values may be sent and summed in bfloat16 or wider, within the bound.
No kernel may reach another device: no remote copies, remote signals or barrier semaphores. Data moves between devices by JAX's collectives and lax.ppermute only.
A program may use at most 128 MiB of HBM per device.

```python
import math
import jax
import jax.numpy as jnp
from jax import lax

CHANNELS = 512
KERNEL_ONE = 10
KERNEL_TWO = 3
CROPS_DEV = 2
SAMPLES = 6400
FRAMES_TWO = 639
ALL_CROPS = 512
N_DP = 64
N_SHARD = 4


def rebalance_plan(key):
    length_key = jax.random.fold_in(key, 11)
    order_key = jax.random.fold_in(key, 13)
    group_size = N_DP * CROPS_DEV
    ranking = jnp.arange(group_size, dtype=jnp.int32)
    rounds = ranking // N_DP
    offset = ranking % N_DP
    holder = jnp.where(rounds % 2 == 0, offset, N_DP - 1 - offset)
    across = (jnp.arange(N_DP, dtype=jnp.int32) + N_DP // 2) % N_DP
    lengths = jnp.zeros((ALL_CROPS,), jnp.int32)
    source = jnp.zeros((ALL_CROPS,), jnp.int32)
    for owner in range(N_SHARD):
        drawn = jnp.minimum(jax.random.randint(jax.random.fold_in(length_key, owner), (group_size,), SAMPLES // 4, SAMPLES + SAMPLES // 2), SAMPLES).astype(jnp.int32)
        ranked = -jnp.sort(-drawn)
        tables = [across]
        for turn in range(1, CROPS_DEV):
            tables.append(jax.random.permutation(jax.random.fold_in(order_key, owner * CROPS_DEV + turn), N_DP).astype(jnp.int32))
        senders = jnp.stack(tables, axis=0)[rounds, holder]
        loaded = (senders * N_SHARD + owner) * CROPS_DEV + rounds
        slots = (holder * N_SHARD + owner) * CROPS_DEV + rounds
        source = source.at[slots].set(loaded)
        lengths = lengths.at[loaded].set(ranked)
    return (lengths, source)


def draw_lengths(key, part):
    return rebalance_plan(key)[0]


def draw_source(key, part):
    return rebalance_plan(key)[1]


def place_ends(result, key, least, top_value):
    place = [jax.random.randint(jax.random.fold_in(key, axis), (), 0, length) for axis, length in enumerate(result.shape)]
    main_axis = result.shape.index(max(result.shape))
    neighbour = place[:main_axis] + [(place[main_axis] + 1) % result.shape[main_axis]] + place[main_axis + 1:]
    return result.at[tuple(place)].set(least).at[tuple(neighbour)].set(top_value)


def shard_levels(stream_key, extent, cuts, smallest, top_value):
    loudness = 1.0
    for position, parts in cuts:
        draws = jax.random.uniform(jax.random.fold_in(jax.random.fold_in(stream_key, 6), position), (parts,), jnp.float32, smallest / len(cuts), top_value / len(cuts))
        loudness = loudness * jnp.repeat(jnp.exp(draws), extent[position] // parts).reshape((-1,) + (1,) * (len(extent) - 1 - position))
    return loudness


def bell_draw(own_key, extent, scale, most, cuts=(), held_as=jnp.bfloat16):
    array = scale * jax.random.normal(own_key, extent, jnp.float32)
    if cuts:
        array = array * shard_levels(own_key, extent, cuts, -0.22, 0.18)
    return jnp.clip(array, -most, most).astype(held_as)


def setup_inputs(seed: int = 0) -> dict:
    arg_keys = jax.random.split(jax.random.key(seed), 12)
    waveform = bell_draw(arg_keys[0], (ALL_CROPS, SAMPLES), 1.0, 6.0, ((0, 256),))
    lengths = draw_lengths(jax.random.fold_in(arg_keys[11], 71), 0)
    source = draw_source(jax.random.fold_in(arg_keys[11], 71), 0)
    frame_mask = place_ends((jax.random.randint(arg_keys[3], (ALL_CROPS, FRAMES_TWO), 0, 5) < 4).astype(jnp.int32), jax.random.fold_in(arg_keys[3], 1), 0, 1)
    cotangent = bell_draw(arg_keys[4], (ALL_CROPS, FRAMES_TWO, CHANNELS), 1.0, 6.0, ((0, 256),))
    conv1_weight = bell_draw(arg_keys[5], (KERNEL_ONE, CHANNELS), KERNEL_ONE ** -0.5, 2.0)
    gain_one = jnp.clip(jnp.exp(jax.random.uniform(arg_keys[6], (CHANNELS,), jnp.float32, math.log(0.5), math.log(2.0))), 0.5, 2.0)
    shift_one = bell_draw(arg_keys[7], (CHANNELS,), 0.5, 3.0, (), jnp.float32)
    conv2_weight = bell_draw(arg_keys[8], (KERNEL_TWO * CHANNELS, CHANNELS), (KERNEL_TWO * CHANNELS) ** -0.5, 0.15625, ((0, 4),))
    gain_two = jnp.clip(jnp.exp(jax.random.uniform(arg_keys[9], (CHANNELS,), jnp.float32, math.log(0.5), math.log(2.0))), 0.5, 2.0)
    shift_two = bell_draw(arg_keys[10], (CHANNELS,), 0.5, 3.0, (), jnp.float32)
    return {"waveform": waveform, "lengths": lengths, "source": source, "frame_mask": frame_mask, "cotangent": cotangent, "conv1_weight": conv1_weight, "gain_one": gain_one, "shift_one": shift_one, "conv2_weight": conv2_weight, "gain_two": gain_two, "shift_two": shift_two}


def gelu_slope(level):
    return 0.5 * (1.0 + jax.scipy.special.erf(level * 0.7071067811865476)) + level * jnp.exp(-0.5 * level * level) * 0.3989422804014327

def layer_norm(values, gain, shift):
    centered = values - lax.optimization_barrier(jnp.mean(values, axis=-1, keepdims=True))
    inverse = lax.rsqrt(lax.optimization_barrier(jnp.mean(centered * centered, axis=-1, keepdims=True)) + 1e-05)
    normed = centered * inverse
    return (normed, inverse, normed * gain + shift)

def norm_back(upward, normed, inverse, gain):
    scaled = upward * gain
    inner = lax.optimization_barrier(jnp.mean(scaled, axis=-1, keepdims=True))
    along = lax.optimization_barrier(jnp.mean(scaled * normed, axis=-1, keepdims=True))
    return inverse * (scaled - inner - normed * along)

def crop_pass(samples, valid, upstream, conv1_weight, gain_one, shift_one, conv2_weight, gain_two, shift_two, loss_scale):
    count, length = samples.shape
    frames_one = length // 5 - 1
    frames_two = length // 10 - 1
    width = conv1_weight.shape[1]
    blocks = samples.reshape(count, length // 5, 5)
    patches = jnp.concatenate([blocks[:, :-1], blocks[:, 1:]], axis=2).reshape(count * frames_one, 10)
    first = jnp.dot(patches, conv1_weight, preferred_element_type=jnp.float32)
    normed_one, inverse_one, level_one = layer_norm(first, gain_one, shift_one)
    hidden = jax.nn.gelu(level_one, approximate=False).astype(jnp.bfloat16).reshape(count, frames_one, width)
    pairs = jnp.concatenate([hidden, jnp.zeros((count, 1, width), jnp.bfloat16)], axis=1).reshape(count, frames_two + 1, 2 * width)
    unfolded = jnp.concatenate([pairs[:, :-1], pairs[:, 1:, :width]], axis=2).reshape(count * frames_two, 3 * width)
    second = jnp.dot(unfolded, conv2_weight, preferred_element_type=jnp.float32)
    normed_two, inverse_two, level_two = layer_norm(second, gain_two, shift_two)
    features = jax.nn.gelu(level_two, approximate=False).astype(jnp.bfloat16).reshape(count, frames_two, width)
    weighting = (valid.reshape(count * frames_two, 1) * loss_scale).astype(jnp.float32)
    up_two = upstream.reshape(count * frames_two, width).astype(jnp.float32) * weighting * gelu_slope(level_two)
    delta_two = norm_back(up_two, normed_two, inverse_two, gain_two).astype(jnp.bfloat16)
    grad_conv = lax.dot_general(unfolded, delta_two, (((0,), (0,)), ((), ())), preferred_element_type=jnp.float32)
    down_unfolded = lax.dot_general(delta_two, conv2_weight, (((1,), (1,)), ((), ())), preferred_element_type=jnp.float32)
    down_unfolded = down_unfolded.reshape(count, frames_two, 3 * width)
    down_pairs = jnp.zeros((count, frames_two + 1, 2 * width), jnp.float32)
    down_pairs = down_pairs.at[:, :-1].add(down_unfolded[:, :, :2 * width])
    down_pairs = down_pairs.at[:, 1:, :width].add(down_unfolded[:, :, 2 * width:])
    down_one = down_pairs.reshape(count, 2 * frames_two + 2, width)[:, :frames_one].reshape(count * frames_one, width)
    up_one = down_one * gelu_slope(level_one)
    delta_one = norm_back(up_one, normed_one, inverse_one, gain_one).astype(jnp.bfloat16)
    grad_taps = lax.dot_general(patches, delta_one, (((0,), (0,)), ((), ())), preferred_element_type=jnp.float32)
    grad_small = jnp.concatenate([grad_taps, lax.optimization_barrier(jnp.sum(up_one * normed_one, axis=0))[None], lax.optimization_barrier(jnp.sum(up_one, axis=0))[None], lax.optimization_barrier(jnp.sum(up_two * normed_two, axis=0))[None], lax.optimization_barrier(jnp.sum(up_two, axis=0))[None]], axis=0)
    return (features, grad_conv, grad_small)

def reference(waveform, lengths, source, frame_mask, cotangent, conv1_weight, gain_one, shift_one, conv2_weight, gain_two, shift_two):
    inside = jnp.arange(SAMPLES, dtype=jnp.int32)[None, :] < lengths[:, None]
    cleaned = jnp.where(inside, waveform, jnp.zeros_like(waveform))
    routed = jnp.take(cleaned, source, axis=0)
    routed_len = jnp.take(lengths, source, axis=0)
    last_sample = 10 * jnp.arange(FRAMES_TWO, dtype=jnp.int32) + 19
    valid = (frame_mask * (last_sample[None, :] < routed_len[:, None]).astype(jnp.int32)).astype(jnp.float32)
    loss_scale = 1.0 / math.sqrt(ALL_CROPS * FRAMES_TWO)

    def one_crop(carry, inputs):
        samples, weighting, upstream = inputs
        features, grad_conv, grad_small = crop_pass(samples[None], weighting[None], upstream[None], conv1_weight, gain_one, shift_one, conv2_weight, gain_two, shift_two, loss_scale)
        return ((carry[0] + grad_conv, carry[1] + grad_small), features[0])
    start = (jnp.zeros((KERNEL_TWO * CHANNELS, CHANNELS), jnp.float32), jnp.zeros((KERNEL_ONE + 4, CHANNELS), jnp.float32))
    totals, features = lax.scan(one_crop, start, (routed, valid, cotangent))
    return (features, totals[0], totals[1])
```

```python
import math

import jax, jax.numpy as jnp
from jax import lax
from jax.experimental import pallas as pl
from jax.experimental.pallas import tpu as pltpu
from jax.sharding import PartitionSpec as P

f32 = jnp.float32
bf = jnp.bfloat16
WIDTH = 512
ROWS = 640
VMEM_LIMIT = 56 * 1024 * 1024


def gelu_parts(y):
    t = 1.0 / (1.0 + 0.23164189 * jnp.abs(y))
    e = jnp.exp2(y * y * (-0.5 * 1.4426950408889634))
    poly = t * (0.127414796 + t * (-0.142248368 + t * (0.7107068705 + t * (-0.7265760135 + t * 0.5307027145))))
    tail = poly * e
    phi = jnp.where(y >= 0, 1.0 - tail, tail)
    return phi, e


def lane_mean(v):
    return jnp.sum(v, axis=-1, keepdims=True) * (1.0 / WIDTH)


def rows8(v):
    return jnp.sum(v.reshape(v.shape[0] // 8, 8, v.shape[1]), axis=0)


TILE = 32
MT = 256


def front_kernel(x_ref, wc_ref, par_ref, w2_ref, cot_ref, fm_ref, len_ref,
                 feat_ref, delta_ref, sg_ref, r1_ref, gw_ref, sums_ref,
                 c_ref, h32_ref, e_ref, o_ref, e1_ref, d32_ref, ds_ref, s_ref):
    total = x_ref.shape[0]
    gain1, shift1, gain2, shift2 = (par_ref[k:k + 1, :] for k in range(4))

    def conv1(i, _):
        r = pl.ds(pl.multiple_of(i * MT, MT), MT)
        c_ref[r, :] = jnp.dot(x_ref[r, :], wc_ref[...], preferred_element_type=f32)
        return 0
    lax.fori_loop(0, total // MT, conv1, 0)
    h32_ref[total:total + 8, :] = jnp.zeros((8, WIDTH), f32)

    def level_one(i, _):
        r = pl.ds(pl.multiple_of(i * TILE, TILE), TILE)
        for half in range(2):
            c = c_ref[r, half * WIDTH:(half + 1) * WIDTH]
            inv = lax.rsqrt(lane_mean(c * c) + 1e-5)
            y = c * inv * gain1 + shift1
            phi, e = gelu_parts(y)
            h = y * phi
            sg_ref[half, r, :] = (phi + (y * 0.3989422804014327) * e) * gain1
            r1_ref[half, r, :] = inv
            if half == 0:
                h32_ref[r, :] = h
                e_ref[r, :] = h.astype(bf)
            else:
                o_ref[r, :] = h.astype(bf)
        return 0
    lax.fori_loop(0, total // TILE, level_one, 0)

    def shift_up(i, _):
        b = pl.multiple_of(i * TILE, TILE)
        e1_ref[pl.ds(b, TILE), :] = h32_ref[pl.ds(b, TILE + 8), :][1:TILE + 1].astype(bf)
        return 0
    lax.fori_loop(0, total // TILE, shift_up, 0)

    def conv2(i, _):
        r = pl.ds(pl.multiple_of(i * MT, MT), MT)
        s_ref[r, :] = (jnp.dot(e_ref[r, :], w2_ref[0:WIDTH, :], preferred_element_type=f32)
                       + jnp.dot(o_ref[r, :], w2_ref[WIDTH:2 * WIDTH, :], preferred_element_type=f32)
                       + jnp.dot(e1_ref[r, :], w2_ref[2 * WIDTH:, :], preferred_element_type=f32))
        return 0
    lax.fori_loop(0, total // MT, conv2, 0)
    d32_ref[0:8, :] = jnp.zeros((8, WIDTH), f32)

    def level_two(i, acc):
        acc_a, acc_b = acc
        b = pl.multiple_of(i * TILE, TILE)
        r = pl.ds(b, TILE)
        z = s_ref[r, :]
        c = z - lane_mean(z)
        inv = lax.rsqrt(lane_mean(c * c) + 1e-5)
        n = c * inv
        y = n * gain2 + shift2
        phi, e = gelu_parts(y)
        feat_ref[r, :] = (y * phi).astype(bf)
        slope = phi + (y * 0.3989422804014327) * e
        crop = b // ROWS
        frame = lax.broadcasted_iota(jnp.int32, (TILE, 1), 0) + (b - crop * ROWS)
        weight = jnp.where(10 * frame + 19 < len_ref[crop], fm_ref[r, :], 0.0)
        up = cot_ref[r, :].astype(f32) * slope * weight
        q = up * gain2
        qn = q * n
        back = inv * (q - lane_mean(q) - n * lane_mean(qn))
        d32_ref[pl.ds(b + 8, TILE), :] = back
        delta_ref[0, r, :] = back.astype(bf)
        return acc_a + rows8(up * n), acc_b + rows8(up)
    zero = jnp.zeros((8, WIDTH), f32)
    acc_a, acc_b = lax.fori_loop(0, total // TILE, level_two, (zero, zero))
    sums_ref[0:8, :] = acc_a
    sums_ref[8:16, :] = acc_b

    def shift_down(i, _):
        b = pl.multiple_of(i * TILE, TILE)
        delta_ref[1, pl.ds(b, TILE), :] = d32_ref[pl.ds(b, TILE + 8), :][7:TILE + 7].astype(bf)
        return 0
    lax.fori_loop(0, total // TILE, shift_down, 0)

    tn = (((0,), (0,)), ((), ()))
    for tap, (lhs, which) in enumerate(((e_ref, 0), (o_ref, 0), (e_ref, 1))):
        for j in range(2):
            gw_ref[tap * WIDTH + j * 256:tap * WIDTH + (j + 1) * 256, :] = lax.dot_general(
                lhs[:, j * 256:(j + 1) * 256], delta_ref[which], tn, preferred_element_type=f32)


def front(x, wc, par, w2, cot, fm, lens):
    total = x.shape[0]
    vm = pl.BlockSpec(memory_space=pltpu.VMEM)
    return pl.pallas_call(
        front_kernel,
        out_shape=(
            jax.ShapeDtypeStruct((total, WIDTH), bf),
            jax.ShapeDtypeStruct((2, total, WIDTH), bf),
            jax.ShapeDtypeStruct((2, total, WIDTH), f32),
            jax.ShapeDtypeStruct((2, total, 1), f32),
            jax.ShapeDtypeStruct((3 * WIDTH, WIDTH), f32),
            jax.ShapeDtypeStruct((16, WIDTH), f32),
        ),
        in_specs=[vm] * 6 + [pl.BlockSpec(memory_space=pltpu.SMEM)],
        out_specs=(vm,) * 6,
        scratch_shapes=[
            pltpu.VMEM((total, 2 * WIDTH), f32),
            pltpu.VMEM((total + 8, WIDTH), f32),
            pltpu.VMEM((total, WIDTH), bf),
            pltpu.VMEM((total, WIDTH), bf),
            pltpu.VMEM((total, WIDTH), bf),
            pltpu.VMEM((total + 8, WIDTH), f32),
            pltpu.VMEM((8, WIDTH), bf),
            pltpu.VMEM((total, WIDTH), f32),
        ],
        compiler_params=pltpu.CompilerParams(vmem_limit_bytes=VMEM_LIMIT),
        name="front",
    )(x, wc, par, w2, cot, fm, lens)


def back_kernel(x_ref, wc_ref, par_ref, w2_ref, delta_ref, sg_ref, r1_ref,
                out_ref, c_ref, d_ref, t_ref):
    total = x_ref.shape[0]
    nt = (((1,), (1,)), ((), ()))
    gain1 = par_ref[0:1, :]

    def mats(i, _):
        r = pl.ds(pl.multiple_of(i * MT, MT), MT)
        c_ref[r, :] = jnp.dot(x_ref[r, :], wc_ref[...], preferred_element_type=f32)
        now = delta_ref[0, r, :]
        d_ref[r, 0:WIDTH] = (lax.dot_general(now, w2_ref[0:WIDTH, :], nt, preferred_element_type=f32)
                             + lax.dot_general(delta_ref[1, r, :], w2_ref[2 * WIDTH:, :], nt, preferred_element_type=f32))
        d_ref[r, WIDTH:] = lax.dot_general(now, w2_ref[WIDTH:2 * WIDTH, :], nt, preferred_element_type=f32)
        return 0
    lax.fori_loop(0, total // MT, mats, 0)

    def level_one(i, acc):
        acc_a, acc_b = acc
        r = pl.ds(pl.multiple_of(i * TILE, TILE), TILE)
        for half in range(2):
            lanes = slice(half * WIDTH, (half + 1) * WIDTH)
            q = d_ref[r, lanes] * sg_ref[half, r, :]
            inv = r1_ref[half, r, :]
            n = c_ref[r, lanes] * inv
            qn = q * n
            t_ref[r, lanes] = (inv * (q - lane_mean(q) - n * lane_mean(qn))).astype(bf)
            acc_a = acc_a + rows8(qn)
            acc_b = acc_b + rows8(q)
        return acc_a, acc_b
    zero = jnp.zeros((8, WIDTH), f32)
    acc_a, acc_b = lax.fori_loop(0, total // TILE, level_one, (zero, zero))
    taps = lax.dot_general(x_ref[:, 0:32], t_ref[...], (((0,), (0,)), ((), ())), preferred_element_type=f32)
    out_ref[0:10, :] = taps[0:10, 0:WIDTH] + taps[5:15, WIDTH:]
    out_ref[10:11, :] = jnp.sum(acc_a, axis=0, keepdims=True) / gain1
    out_ref[11:12, :] = jnp.sum(acc_b, axis=0, keepdims=True) / gain1
    out_ref[12:16, :] = jnp.zeros((4, WIDTH), f32)


def back(x, wc, par, w2, delta, sg, r1):
    total = x.shape[0]
    vm = pl.BlockSpec(memory_space=pltpu.VMEM)
    return pl.pallas_call(
        back_kernel,
        out_shape=jax.ShapeDtypeStruct((16, WIDTH), f32),
        in_specs=[vm] * 7,
        out_specs=vm,
        scratch_shapes=[
            pltpu.VMEM((total, 2 * WIDTH), f32),
            pltpu.VMEM((total, 2 * WIDTH), f32),
            pltpu.VMEM((total, 2 * WIDTH), bf),
        ],
        compiler_params=pltpu.CompilerParams(vmem_limit_bytes=VMEM_LIMIT),
        name="back",
    )(x, wc, par, w2, delta, sg, r1)


def prep_weights(conv1_weight):
    w1 = conv1_weight.astype(f32)
    wc = w1 - jnp.mean(w1, axis=1, keepdims=True)
    z5 = jnp.zeros((5, WIDTH), f32)
    z10 = jnp.zeros((10, WIDTH), f32)
    both = jnp.concatenate([jnp.concatenate([wc, z10], 0), jnp.concatenate([z5, wc, z5], 0)], 1)
    hi = lax.reduce_precision(both, 8, 7)
    mid = lax.reduce_precision(both - hi, 8, 7)
    low = both - hi - mid
    return jnp.concatenate([hi.astype(bf), mid.astype(bf), low.astype(bf)], 0)


def unfold(samples):
    count, length = samples.shape
    flat = samples.reshape(count, length // 10, 10)
    nxt = jnp.concatenate([flat[:, 1:], jnp.zeros((count, 1, 10), bf)], 1)
    x = jnp.concatenate([flat, nxt], 2).reshape(count * length // 10, 20)
    return jnp.concatenate([x, x, x], 1)


def ring(n_all, stride, n, k):
    pairs = []
    for i in range(n_all):
        at = i // stride % n
        pairs.append((i, i + ((at + k) % n - at) * stride))
    return pairs


def flip(n_all, stride, bit):
    return [(i, i ^ (bit * stride)) for i in range(n_all)]


Y, Z, C, X = 4, 8, 2, 4
DP = Y * Z * C
CORE = flip(DP, 1, 1)
YZ_GROUPS = [[yz * C + c for yz in range(Y * Z)] for c in range(C)]


def route(waveform, lengths, source):
    count, length = waveform.shape
    me = lax.axis_index("dp")
    y, z, c = me // (Z * C), me // C % Z, me % C
    wanted_peer = lax.ppermute(source, "dp", CORE)
    inside = jnp.arange(length, dtype=jnp.int32)[None, :] < lengths[:, None]
    cleaned = jnp.where(inside, waveform, jnp.zeros_like(waveform))
    tail = jnp.stack([lengths // 128, lengths % 128], 1).astype(bf)
    tail = jnp.pad(tail, ((0, 0), (0, 126)))
    own = jnp.concatenate([cleaned, tail], 1)
    pair = jnp.concatenate([own, lax.ppermute(own, "dp", flip(DP, C, 1))], 0)
    plane = jnp.concatenate(
        [pair] + [lax.ppermute(pair, "dp", ring(DP, C, Z, k)) for k in (2, 4, 6)], 0)
    planes = [plane] + [lax.ppermute(plane, "dp", ring(DP, Z * C, Y, k)) for k in (1, 3, 2)]
    order = (0, 1, 3, 2)

    def pick(crop):
        holder = crop // count // X
        ys, zs = holder // (Z * C), holder // C % Z
        row = ((z // 2 - zs // 2) % 4 * 2 + (z + zs) % 2) * count + crop % count
        step = (y - ys) % Y
        out = None
        for k, block in zip(order, planes):
            part = lax.dynamic_slice_in_dim(block, row, 1, 0)
            out = part if out is None else jnp.where(step == k, part, out)
        return out

    mine = jnp.concatenate([pick(source[i]) for i in range(count)], 0)
    theirs = jnp.concatenate([pick(wanted_peer[i]) for i in range(count)], 0)
    got = lax.ppermute(theirs, "dp", CORE)
    local = (source // count // X % C == c)[:, None]
    routed = jnp.where(local, mine, got)
    coded = routed[:, length:length + 2].astype(jnp.int32)
    return routed[:, :length], coded[:, 0] * 128 + coded[:, 1]


def reduce_grads(gw, back_terms, sums):
    me = lax.axis_index("dp")
    c, x = me % C, lax.axis_index("shard")
    part = gw.shape[0] // (C * X)
    split = gw.reshape(X, C, part, WIDTH)
    away = lax.dynamic_index_in_dim(split, 1 - c, 1, False).astype(bf)
    here = lax.dynamic_index_in_dim(split, c, 1, False)
    here = here + lax.ppermute(away, "dp", CORE).astype(f32)
    total = lax.dynamic_index_in_dim(here, x, 0, False)
    for k in (1, 3, 2):
        piece = lax.dynamic_index_in_dim(here, (x + k) % X, 0, False).astype(bf)
        total = total + lax.ppermute(piece, "shard", ring(X, 1, X, k)).astype(f32)
    lanes = WIDTH // 128
    chunk = total.reshape(part, lanes, 128).transpose(1, 0, 2).reshape(Y * Z, -1, 128)
    small = jnp.concatenate(
        [back_terms[:12], jnp.sum(sums.reshape(2, 8, WIDTH), axis=1), jnp.zeros((2, WIDTH), f32)], 0)
    rows = small.shape[0] * lanes // (Y * Z)
    small = small.reshape(Y * Z, rows, 128)
    chunk = jnp.concatenate([chunk, small], 1).astype(bf)
    got = lax.all_to_all(chunk, "dp", 0, 0, axis_index_groups=YZ_GROUPS, tiled=True)
    summed = jnp.sum(got.astype(f32), axis=0).astype(bf)
    every = lax.all_to_all(
        jnp.broadcast_to(summed[None], chunk.shape), "dp", 0, 0, axis_index_groups=YZ_GROUPS, tiled=True)
    half = every[:, :-rows].reshape(lanes, part, 128).transpose(1, 0, 2).reshape(part, WIDTH)
    other = lax.ppermute(half, "dp", CORE)
    grad_conv2 = jnp.where(c == 0, jnp.concatenate([half, other], 0), jnp.concatenate([other, half], 0)).astype(f32)
    small = every[:, -rows:].astype(f32).reshape(-1, WIDTH)
    small = small + lax.ppermute(small, "dp", CORE)
    a, b, d = (lax.ppermute(small, "shard", flip(X, 1, k)) for k in (1, 2, 3))
    small = (small + a) + (b + d)
    return grad_conv2, small[:14]


def body(waveform, lengths, source, frame_mask, cotangent, conv1_weight, gain_one, shift_one,
         conv2_weight, gain_two, shift_two):
    count, frames = frame_mask.shape
    w2 = lax.all_gather(conv2_weight, "shard", axis=0, tiled=True)
    loss_scale = 1.0 / math.sqrt(count * DP * X * frames)
    upstream = jnp.pad(cotangent, ((0, 0), (0, 1), (0, 0))).reshape(count * ROWS, WIDTH)
    weights = jnp.pad(frame_mask.astype(f32) * loss_scale, ((0, 0), (0, 1))).reshape(count * ROWS, 1)
    par = jnp.concatenate(
        [jnp.stack([gain_one, shift_one, gain_two, shift_two]), jnp.zeros((4, WIDTH), f32)], 0)
    wc = prep_weights(conv1_weight)
    samples, lens = route(waveform, lengths, source)
    patches = unfold(samples)
    feat, delta, slope, inverse, gw, sums = front(patches, wc, par, w2, upstream, weights, lens)
    back_terms = back(patches, wc, par, w2, delta, slope, inverse)
    grad_conv2, grad_front = reduce_grads(gw, back_terms, sums)
    features = feat.reshape(count, ROWS, WIDTH)[:, :frames]
    return features, grad_conv2, grad_front


def solution(mesh):
    both = P(("dp", "shard"))
    placed = (both, both, both, both, both, P(), P(), P(), P("shard"), P(), P())
    return jax.shard_map(
        body,
        mesh=mesh,
        in_specs=placed,
        out_specs=(both, P("shard"), P()),
        check_vma=False,
    )
```

```python
import math

import jax
import jax.numpy as jnp
from jax import lax
from jax.experimental import pallas as pl
from jax.experimental.pallas import tpu as pltpu
from jax.sharding import PartitionSpec as P

f32 = jnp.float32
bf = jnp.bfloat16
WIDTH = 512
HALF = 256
ROWS = 640
VMEM_LIMIT = 60 * 1024 * 1024
T1, T2, T3 = 128, 256, 256
M1, M2, M3, MG = 256, 1280, 640, 512
NN = (((1,), (0,)), ((), ()))
NT = (((1,), (1,)), ((), ()))
TN = (((0,), (0,)), ((), ()))


def gelu_parts(y):
    d = 1.0 + 0.23164189 * jnp.abs(y)
    t = pl.reciprocal(d, approx=True)
    t = t * (2.0 - d * t)
    e = jnp.exp2(y * (y * (-0.5 * 1.4426950408889634)))
    poly = t * (0.127414796 + t * (-0.142248368 + t * (0.7107068705 + t * (-0.7265760135 + t * 0.5307027145))))
    tail = poly * e
    return jnp.where(y >= 0, 1.0 - tail, tail), e


def lane_sum(v):
    return jnp.sum(v, axis=-1, keepdims=True)


def rows8(v):
    return jnp.sum(v.reshape(v.shape[0] // 8, 8, v.shape[1]), axis=0)


def dot(a, b, dims=NN):
    return lax.dot_general(a, b, dims, preferred_element_type=f32)


def shifted_up(v, below):
    return jnp.concatenate([v, below], 0)[1:v.shape[0] + 1]


def shifted_down(v, above):
    return jnp.concatenate([above, v], 0)[7:v.shape[0] + 7]


def norm_back(q, n, inv):
    qn = q * n
    inner = lane_sum(q) * (1.0 / WIDTH)
    along = lane_sum(qn) * (1.0 / WIDTH)
    return inv * (q - inner - n * along), qn


def encoder_kernel(ids_ref, x_ref, wc_ref, par_ref, fm_ref, tail_ref, cot_hbm, wa_hbm, wb_hbm, wc_hbm, wd_hbm,
                   feat_ref, keep_ref, send_ref,
                   w2_ref, cot_ref, sems, p_ref, small_ref, c_ref, u_ref, s_ref, d_ref, sg_ref, r1_ref, dl_ref, t_ref):
    total = x_ref.shape[0]
    core = ids_ref[0]
    part = wa_hbm.shape[0]
    loads = []
    for k, src in enumerate((wa_hbm, wb_hbm, wc_hbm, wd_hbm)):
        at = pl.multiple_of((ids_ref[1] ^ k) * part, part)
        loads.append(pltpu.make_async_copy(src, w2_ref.at[pl.ds(at, part), :], sems.at[k]))
    loads.append(pltpu.make_async_copy(cot_hbm, cot_ref, sems.at[4]))
    for load in loads:
        load.start()
    gain1, shift1, gain2, shift2 = (par_ref[k:k + 1, :] for k in range(4))
    zero = jnp.zeros((8, WIDTH), f32)
    tail = tail_ref[...].astype(f32)
    length = tail[:, 0:1] * 128.0 + tail[:, 1:2]

    def rows(i, size):
        return pl.ds(pl.multiple_of(i * size, size), size)

    now = x_ref[...].astype(f32)
    later = shifted_up(now, jnp.zeros((8, now.shape[1]), f32))
    k = lax.broadcasted_iota(jnp.int32, (10, 128), 0)
    lane = lax.broadcasted_iota(jnp.int32, (10, 128), 1)
    step = lane - lane // 20 * 20
    used = lane < 60
    place = jnp.where(used & (step == k), 1.0, 0.0).astype(bf)
    place_later = jnp.where(used & (step == k + 10), 1.0, 0.0).astype(bf)
    p_ref[...] = (dot(now.astype(bf), place) + dot(later.astype(bf), place_later)).astype(bf)

    def conv1(i, _):
        r = rows(i, M1)
        c_ref[r, :] = dot(p_ref[r, 0:64], wc_ref[...])
        return 0
    lax.fori_loop(0, total // M1, conv1, 0)

    def level_one(i, below):
        r = rows(total // T1 - 1 - i, T1)
        for half in range(2):
            c = c_ref[r, half * WIDTH:(half + 1) * WIDTH]
            inv = lax.rsqrt(lane_sum(c * c) * (1.0 / WIDTH) + 1e-5)
            y = c * inv * gain1 + shift1
            phi, e = gelu_parts(y)
            h = y * phi
            sg_ref[half, r, :] = (phi + (y * 0.3989422804014327) * e) * gain1
            r1_ref[half, r, :] = inv
            u_ref[r, half * WIDTH:(half + 1) * WIDTH] = h.astype(bf)
            if half == 0:
                u_ref[r, 2 * WIDTH:] = shifted_up(h, below).astype(bf)
                first = h[0:8]
        return first
    lax.fori_loop(0, total // T1, level_one, zero)

    for load in loads[:4]:
        load.wait()

    def conv2(i, _):
        r = rows(i, M2)
        s_ref[r, :] = dot(u_ref[r, :], w2_ref[...])
        return 0
    lax.fori_loop(0, total // M2, conv2, 0)

    loads[4].wait()

    def level_two(i, carry):
        acc_a, acc_b, above = carry
        b = pl.multiple_of(i * T2, T2)
        r = pl.ds(b, T2)
        z = s_ref[r, :]
        c = z - lane_sum(z) * (1.0 / WIDTH)
        inv = lax.rsqrt(lane_sum(c * c) * (1.0 / WIDTH) + 1e-5)
        n = c * inv
        y = n * gain2 + shift2
        phi, e = gelu_parts(y)
        feat_ref[r, :] = (y * phi).astype(bf)
        slope = phi + (y * 0.3989422804014327) * e
        row = (lax.broadcasted_iota(jnp.int32, (T2, 1), 0) + b).astype(f32)
        room = jnp.where(row < ROWS, length[0:1], length[1:2] + 10.0 * ROWS)
        weight = jnp.where(10.0 * row + 19.0 < room, fm_ref[r, :], 0.0)
        q = cot_ref[r, :].astype(f32) * weight * (slope * gain2)
        back, qn = norm_back(q, n, inv)
        dl_ref[r, 0:WIDTH] = back.astype(bf)
        dl_ref[r, WIDTH:] = shifted_down(back, above).astype(bf)
        return acc_a + rows8(qn), acc_b + rows8(q), back[T2 - 8:T2]
    acc_a, acc_b, _ = lax.fori_loop(0, total // T2, level_two, (zero, zero, zero))
    small_ref[12:13, :] = jnp.sum(acc_a, axis=0, keepdims=True) / gain2
    small_ref[13:14, :] = jnp.sum(acc_b, axis=0, keepdims=True) / gain2
    small_ref[14:16, :] = jnp.zeros((2, WIDTH), f32)

    for ref, half in ((keep_ref, core), (send_ref, 1 - core)):
        for tap, shift in ((0, 0), (1, 0), (0, WIDTH)):
            base = (tap if shift == 0 else 2) * WIDTH
            cols = pl.ds(pl.multiple_of(shift + half * HALF, HALF), HALF)
            ref[base:base + WIDTH, :] = dot(u_ref[:, tap * WIDTH:(tap + 1) * WIDTH], dl_ref[:, cols], TN).astype(ref.dtype)

    def down(i, _):
        r = rows(i, M3)
        now = dl_ref[r, 0:WIDTH]
        s_ref[r, :] = dot(now, w2_ref[0:WIDTH, :], NT) + dot(dl_ref[r, WIDTH:], w2_ref[2 * WIDTH:, :], NT)
        d_ref[r, :] = dot(now, w2_ref[WIDTH:2 * WIDTH, :], NT)
        return 0
    lax.fori_loop(0, total // M3, down, 0)

    def level_one_back(i, acc):
        acc_a, acc_b = acc
        r = rows(i, T3)
        for half, down_ref in enumerate((s_ref, d_ref)):
            lanes = slice(half * WIDTH, (half + 1) * WIDTH)
            q = down_ref[r, :] * sg_ref[half, r, :]
            inv = r1_ref[half, r, :]
            back, qn = norm_back(q, c_ref[r, lanes] * inv, inv)
            t_ref[r, lanes] = back.astype(bf)
            acc_a = acc_a + rows8(qn)
            acc_b = acc_b + rows8(q)
        return acc_a, acc_b
    acc_a, acc_b = lax.fori_loop(0, total // T3, level_one_back, (zero, zero))
    small_ref[10:11, :] = jnp.sum(acc_a, axis=0, keepdims=True) / gain1
    small_ref[11:12, :] = jnp.sum(acc_b, axis=0, keepdims=True) / gain1
    taps = dot(p_ref[:, 0:32], t_ref[...], TN)
    small_ref[0:10, :] = taps[0:10, 0:WIDTH] + taps[5:15, WIDTH:]
    small = small_ref[...].astype(bf)
    for j in range(2):
        r = slice(3 * WIDTH + 16 * j, 3 * WIDTH + 16 * (j + 1))
        send_ref[r, :] = small[:, j * HALF:(j + 1) * HALF]
        keep_ref[r, :] = small[:, j * HALF:(j + 1) * HALF].astype(f32)


def encoder(ids, x, wc, par, fm, tail, cot, parts):
    total = x.shape[0]
    vm = pl.BlockSpec(memory_space=pltpu.VMEM)
    hbm = pl.BlockSpec(memory_space=pl.ANY)
    return pl.pallas_call(
        encoder_kernel,
        out_shape=(
            jax.ShapeDtypeStruct((total, WIDTH), bf),
            jax.ShapeDtypeStruct((3 * WIDTH + 32, HALF), f32),
            jax.ShapeDtypeStruct((3 * WIDTH + 32, HALF), bf),
        ),
        in_specs=[pl.BlockSpec(memory_space=pltpu.SMEM)] + [vm] * 5 + [hbm] * 5,
        out_specs=(vm,) * 3,
        scratch_shapes=[
            pltpu.VMEM((3 * WIDTH, WIDTH), bf),
            pltpu.VMEM((total, WIDTH), bf),
            pltpu.SemaphoreType.DMA((5,)),
            pltpu.VMEM((total, 128), bf),
            pltpu.VMEM((16, WIDTH), f32),
            pltpu.VMEM((total, 2 * WIDTH), f32),
            pltpu.VMEM((total, 3 * WIDTH), bf),
            pltpu.VMEM((total, WIDTH), f32),
            pltpu.VMEM((total, WIDTH), f32),
            pltpu.VMEM((2, total, WIDTH), f32),
            pltpu.VMEM((2, total, 1), f32),
            pltpu.VMEM((total, 2 * WIDTH), bf),
            pltpu.VMEM((total, 2 * WIDTH), bf),
        ],
        compiler_params=pltpu.CompilerParams(vmem_limit_bytes=VMEM_LIMIT),
        name="encoder",
    )(ids, x, wc, par, fm, tail, cot, *parts)


def prep_weights(conv1_weight):
    w1 = conv1_weight.astype(f32)
    wc = w1 - jnp.mean(w1, axis=1, keepdims=True)
    z5 = jnp.zeros((5, WIDTH), f32)
    z10 = jnp.zeros((10, WIDTH), f32)
    both = jnp.concatenate([jnp.concatenate([wc, z10], 0), jnp.concatenate([z5, wc, z5], 0)], 1)
    hi = lax.reduce_precision(both, 8, 7)
    mid = lax.reduce_precision(both - hi, 8, 7)
    low = both - hi - mid
    return jnp.concatenate([hi.astype(bf), mid.astype(bf), low.astype(bf), jnp.zeros((4, 2 * WIDTH), bf)], 0)


Y, Z, C, X = 4, 8, 2, 4
DP = Y * Z * C
CORE = [(i, i ^ 1) for i in range(DP)]
YZ_GROUPS = [[yz * C + c for yz in range(Y * Z)] for c in range(C)]


def flip(k):
    return [(i, i ^ k) for i in range(X)]


def exchange(chunks):
    return lax.all_to_all(chunks, "dp", 0, 0, axis_index_groups=YZ_GROUPS, tiled=True)


def pack(waveform, lengths):
    count, length = waveform.shape
    inside = jnp.arange(length, dtype=jnp.int32)[None, :] < lengths[:, None]
    cleaned = jnp.where(inside, waveform, jnp.zeros_like(waveform))
    tail = jnp.stack([lengths >> 7, lengths & 127], 1).astype(bf)
    return jnp.concatenate([cleaned, jnp.pad(tail, ((0, 0), (0, 126)))], 1)


def pick(source, column, other_column, core):
    count, holder = source.shape[0], source >> 3
    local = (holder & 1) == core
    crops = []
    for i in range(count):
        start = (holder[i] >> 1, source[i] & 1, 0)
        size = (1, 1, column.shape[2])
        crops.append(jnp.where(local[i], lax.dynamic_slice(column, start, size),
                               lax.dynamic_slice(other_column, start, size))[0])
    return jnp.concatenate(crops, 0)


def gather_weight(weight):
    return [weight] + [lax.ppermute(weight, "shard", flip(k)) for k in (1, 2, 3)]


def reduce_grads(keep, send, core, shadow):
    x = lax.axis_index("shard")
    part = 3 * WIDTH // X
    here = keep + lax.ppermute(send, "dp", CORE).astype(f32)
    small = here[3 * WIDTH:].astype(bf)
    here, shadow = lax.optimization_barrier((here, shadow))

    def piece(k):
        return lax.dynamic_slice_in_dim(here, (x ^ k) * part, part, 0)
    got = [lax.ppermute(jnp.concatenate([piece(k).astype(bf), small], 0), "shard", flip(k)).astype(f32)
           for k in (1, 2, 3)]
    total = (jnp.concatenate([piece(0), small.astype(f32)], 0) + got[0]) + (got[1] + got[2])
    lanes = HALF // 128
    chunk = total.astype(bf).reshape(-1, lanes, 128).transpose(1, 0, 2).reshape(Y * Z, -1, 128)
    summed = jnp.sum(exchange(chunk).astype(f32), axis=0).astype(bf)
    every = exchange(jnp.broadcast_to(summed[None], chunk.shape))
    every = every.reshape(lanes, -1, 128).transpose(1, 0, 2).reshape(-1, HALF)
    half = every[:part]
    other = lax.ppermute(half, "dp", CORE)
    grad_conv2 = jnp.where(core == 0, jnp.concatenate([half, other], 1), jnp.concatenate([other, half], 1))
    small = jnp.concatenate([every[part:part + 14], every[part + 16:part + 30]], 1)
    return grad_conv2.astype(f32), small.astype(f32), shadow


def body(waveform, lengths, source, frame_mask, cotangent, conv1_weight, gain_one, shift_one,
         conv2_weight, gain_two, shift_two):
    count, frames = frame_mask.shape
    core, x = lax.axis_index("dp") & 1, lax.axis_index("shard")
    parts = gather_weight(conv2_weight)
    loss_scale = 1.0 / math.sqrt(count * DP * X * frames)
    upstream = jnp.pad(cotangent, ((0, 0), (0, 1), (0, 0))).reshape(count * ROWS, WIDTH)
    weights = jnp.pad(frame_mask.astype(f32) * loss_scale, ((0, 0), (0, 1))).reshape(count * ROWS, 1)
    par = jnp.concatenate(
        [jnp.stack([gain_one, shift_one, gain_two, shift_two]), jnp.zeros((4, WIDTH), f32)], 0)
    wc = prep_weights(conv1_weight)
    own = pack(waveform, lengths)
    column = exchange(jnp.broadcast_to(own[None], (Y * Z,) + own.shape))
    routed = pick(source, column, lax.ppermute(column, "dp", CORE), core)
    length = waveform.shape[1]
    blocks = routed[:, :length].reshape(count * ROWS, 10)
    feat, keep, send = encoder(
        jnp.stack([core, x]), blocks, wc, par, weights, routed[:, length:], upstream, parts)
    features = feat.reshape(count, ROWS, WIDTH)[:, :frames]
    grad_conv2, grad_front, features = reduce_grads(keep, send, core, features)
    return features, grad_conv2, grad_front


def solution(mesh):
    both = P(("dp", "shard"))
    placed = (both, both, both, both, both, P(), P(), P(), P("shard"), P(), P())
    return jax.shard_map(
        body,
        mesh=mesh,
        in_specs=placed,
        out_specs=(both, P("shard"), P()),
        check_vma=False,
    )
```

```python
import math

import jax
import jax.numpy as jnp
from jax import lax
from jax.experimental import pallas as pl
from jax.experimental.pallas import tpu as pltpu
from jax.sharding import Mesh
from jax.sharding import PartitionSpec as P

f32 = jnp.float32
bf = jnp.bfloat16
WIDTH = 512
HALF = 256
ROWS = 640
SAMPLES = 6400
LOSS_SCALE = 1.0 / math.sqrt(512 * 639)
PART = 96
SLOTS = PART + 16
VMEM_LIMIT = 60 * 1024 * 1024
M1, TA, TB, TC = 256, 256, 256, 320
NN = (((1,), (0,)), ((), ()))
NT = (((1,), (1,)), ((), ()))
TN = (((0,), (0,)), ((), ()))


def gelu_parts(y):
    d = 1.0 + 0.23164189 * jnp.abs(y)
    t = pl.reciprocal(d, approx=True)
    t = t * (2.0 - d * t)
    e = jnp.exp2(y * (y * (-0.5 * 1.4426950408889634)))
    poly = t * (0.127414796 + t * (-0.142248368 + t * (0.7107068705 + t * (-0.7265760135 + t * 0.5307027145))))
    tail = poly * e
    return jnp.where(y >= 0, 1.0 - tail, tail), e


def lane_sum(v):
    return jnp.sum(v, axis=-1, keepdims=True)


def rows8(v):
    return jnp.sum(v.reshape(v.shape[0] // 8, 8, v.shape[1]), axis=0)


def dot(a, b, dims=NN):
    return lax.dot_general(a, b, dims, preferred_element_type=f32)


def shifted_up(v, below):
    return jnp.concatenate([v, below], 0)[1:v.shape[0] + 1]


def shifted_down(v, above):
    return jnp.concatenate([above, v], 0)[7:v.shape[0] + 7]


def norm_back(q, n, inv):
    qn = q * n
    inner = lane_sum(q) * (1.0 / WIDTH)
    along = lane_sum(qn) * (1.0 / WIDTH)
    return inv * (q - inner - n * along), qn


def encoder_kernel(ids_ref, x_ref, wc_ref, par_ref, tail_ref, cot_hbm, wa_hbm, wb_hbm, wc_hbm, wd_hbm,
                   feat_ref, keep_ref, send_ref,
                   w2_ref, cot_ref, sems, p_ref, small_ref, c_ref, u_ref, s_ref, d_ref, sg_ref, r1_ref, dl_ref, t_ref):
    total = x_ref.shape[0]
    core = ids_ref[0]
    part = wa_hbm.shape[0]
    loads = []
    for k, src in enumerate((wa_hbm, wb_hbm, wc_hbm, wd_hbm)):
        at = pl.multiple_of((ids_ref[1] ^ k) * part, part)
        loads.append(pltpu.make_async_copy(src, w2_ref.at[pl.ds(at, part), :], sems.at[k]))
    loads.append(pltpu.make_async_copy(cot_hbm, cot_ref, sems.at[4]))
    for load in loads:
        load.start()
    gain1, shift1, gain2, shift2 = (par_ref[k:k + 1, :] for k in range(4))
    zero = jnp.zeros((8, WIDTH), f32)
    tail = tail_ref[:, SAMPLES:].astype(f32)
    length = tail[:, 0:1] * 128.0 + tail[:, 1:2]

    def rows(i, size):
        return pl.ds(pl.multiple_of(i * size, size), size)

    now = x_ref[...].astype(f32)
    later = shifted_up(now, jnp.zeros((8, now.shape[1]), f32))
    k = lax.broadcasted_iota(jnp.int32, (10, 128), 0)
    lane = lax.broadcasted_iota(jnp.int32, (10, 128), 1)
    step = lane - lane // 20 * 20
    used = lane < 60
    place = jnp.where(used & (step == k), 1.0, 0.0).astype(bf)
    place_later = jnp.where(used & (step == k + 10), 1.0, 0.0).astype(bf)
    p_ref[...] = (dot(now.astype(bf), place) + dot(later.astype(bf), place_later)).astype(bf)

    def conv1(i, _):
        r = rows(i, M1)
        c_ref[r, :] = dot(p_ref[r, 0:64], wc_ref[...])
        return 0
    lax.fori_loop(0, total // M1, conv1, 0)

    def level_one(t, below):
        r = rows(t, TA)
        for half in range(2):
            c = c_ref[r, half * WIDTH:(half + 1) * WIDTH]
            inv = lax.rsqrt(lane_sum(c * c) * (1.0 / WIDTH) + 1e-5)
            y = c * inv * gain1 + shift1
            phi, e = gelu_parts(y)
            h = y * phi
            sg_ref[half, r, :] = (phi + (y * 0.3989422804014327) * e) * gain1
            r1_ref[half, r, :] = inv
            u_ref[r, half * WIDTH:(half + 1) * WIDTH] = h.astype(bf)
            if half == 0:
                u_ref[r, 2 * WIDTH:] = shifted_up(h, below).astype(bf)
                first = h[0:8]
        return first

    def conv2(t):
        r = rows(t, TA)
        s_ref[r, :] = dot(u_ref[r, :], w2_ref[...])

    def forward(i, below):
        t = total // TA - 2 - i
        conv2(t + 1)
        return level_one(t, below)
    below = level_one(total // TA - 1, zero)
    for load in loads[:4]:
        load.wait()
    lax.fori_loop(0, total // TA - 1, forward, below)
    conv2(0)

    loads[4].wait()

    def level_two(t, carry):
        acc_a, acc_b, above = carry
        b = pl.multiple_of(t * TB, TB)
        r = pl.ds(b, TB)
        z = s_ref[r, :]
        c = z - lane_sum(z) * (1.0 / WIDTH)
        inv = lax.rsqrt(lane_sum(c * c) * (1.0 / WIDTH) + 1e-5)
        n = c * inv
        y = n * gain2 + shift2
        phi, e = gelu_parts(y)
        feat_ref[r, :] = (y * phi).astype(bf)
        slope = phi + (y * 0.3989422804014327) * e
        row = (lax.broadcasted_iota(jnp.int32, (TB, 1), 0) + b).astype(f32)
        room = jnp.where(row < ROWS, length[0:1], length[1:2] + 10.0 * ROWS)
        weight = jnp.where(10.0 * row + 19.0 < room, LOSS_SCALE, 0.0)
        q = cot_ref[r, :].astype(f32) * weight * (slope * gain2)
        back, qn = norm_back(q, n, inv)
        dl_ref[r, 0:WIDTH] = back.astype(bf)
        dl_ref[r, WIDTH:] = shifted_down(back, above).astype(bf)
        return acc_a + rows8(qn), acc_b + rows8(q), back[TB - 8:TB]

    def down(t):
        r = rows(t, TB)
        now = dl_ref[r, 0:WIDTH]
        d_ref[r, 0:WIDTH] = dot(now, w2_ref[0:WIDTH, :], NT) + dot(dl_ref[r, WIDTH:], w2_ref[2 * WIDTH:, :], NT)
        d_ref[r, WIDTH:] = dot(now, w2_ref[WIDTH:2 * WIDTH, :], NT)

    def middle(t, carry):
        down(t - 1)
        return level_two(t, carry)
    carry = level_two(0, (zero, zero, zero))
    acc_a, acc_b, _ = lax.fori_loop(1, total // TB, middle, carry)
    down(total // TB - 1)
    small_ref[12:13, :] = jnp.sum(acc_a, axis=0, keepdims=True) / gain2
    small_ref[13:14, :] = jnp.sum(acc_b, axis=0, keepdims=True) / gain2
    small_ref[14:16, :] = jnp.zeros((2, WIDTH), f32)

    def backward(i, acc):
        acc_a, acc_b = acc
        chunk = 3 * WIDTH // (total // TC)
        for ref, half in ((keep_ref, core), (send_ref, 1 - core)):
            cols = pl.ds(pl.multiple_of(half * HALF, HALF), HALF)
            grad = dot(u_ref[:, pl.ds(pl.multiple_of(i * chunk, chunk), chunk)], dl_ref[:, cols], TN).astype(ref.dtype)
            for j in range(4):
                ref[4 * j + i, 0:PART, :] = grad[j * PART:(j + 1) * PART]
        r = rows(i, TC)
        for half in range(2):
            lanes = slice(half * WIDTH, (half + 1) * WIDTH)
            q = d_ref[r, lanes] * sg_ref[half, r, :]
            inv = r1_ref[half, r, :]
            back, qn = norm_back(q, c_ref[r, lanes] * inv, inv)
            t_ref[r, lanes] = back.astype(bf)
            acc_a = acc_a + rows8(qn)
            acc_b = acc_b + rows8(q)
        return acc_a, acc_b
    acc_a, acc_b = lax.fori_loop(0, total // TC, backward, (zero, zero))
    small_ref[10:11, :] = jnp.sum(acc_a, axis=0, keepdims=True) / gain1
    small_ref[11:12, :] = jnp.sum(acc_b, axis=0, keepdims=True) / gain1
    taps = dot(p_ref[:, 0:32], t_ref[...], TN)
    small_ref[0:10, :] = taps[0:10, 0:WIDTH] + taps[5:15, WIDTH:]
    small = small_ref[...].astype(bf)
    for j in range(4):
        quarter = jnp.concatenate([small[:, 128 * j:128 * (j + 1)], jnp.zeros((16, 128), bf)], 1)
        for i in range(4):
            send_ref[4 * j + i, PART:SLOTS, :] = quarter
            keep_ref[4 * j + i, PART:SLOTS, :] = quarter.astype(f32)


def pick_kernel(ids_ref, source_ref, own_hbm, other_hbm, out_ref, slab_ref, sems):
    for i in range(2):
        holder = source_ref[i] >> 3
        local = (holder & 1) == ids_ref[0]

        @pl.when(local)
        def _():
            pltpu.make_async_copy(own_hbm.at[holder >> 1], slab_ref.at[i], sems.at[i]).start()

        @pl.when(jnp.logical_not(local))
        def _():
            pltpu.make_async_copy(other_hbm.at[holder >> 1], slab_ref.at[i], sems.at[i]).start()
    crops = []
    for i in range(2):
        pltpu.make_async_copy(own_hbm.at[0], slab_ref.at[i], sems.at[i]).wait()
        both = slab_ref[i].astype(f32)
        crops.append(jnp.where((source_ref[i] & 1) == 0, both[0:1], both[1:2]))
    row = lax.broadcasted_iota(jnp.int32, out_ref.shape, 0)
    out_ref[...] = jnp.where(row == 0, crops[0], crops[1]).astype(bf)


def pick(ids, source, own, other):
    smem, hbm = pl.BlockSpec(memory_space=pltpu.SMEM), pl.BlockSpec(memory_space=pl.ANY)
    shape = own.shape[1:]
    return pl.pallas_call(
        pick_kernel,
        out_shape=jax.ShapeDtypeStruct(shape, bf),
        in_specs=[smem, smem, hbm, hbm],
        out_specs=pl.BlockSpec(memory_space=pltpu.VMEM),
        scratch_shapes=[pltpu.VMEM((2,) + shape, bf), pltpu.SemaphoreType.DMA((2,))],
        name="pick",
    )(ids, source, own, other)


def encoder(ids, x, wc, par, tail, cot, parts):
    total = x.shape[0]
    vm = pl.BlockSpec(memory_space=pltpu.VMEM)
    hbm = pl.BlockSpec(memory_space=pl.ANY)
    return pl.pallas_call(
        encoder_kernel,
        out_shape=(
            jax.ShapeDtypeStruct((total, WIDTH), bf),
            jax.ShapeDtypeStruct((16, SLOTS, HALF), f32),
            jax.ShapeDtypeStruct((16, SLOTS, HALF), bf),
        ),
        in_specs=[pl.BlockSpec(memory_space=pltpu.SMEM)] + [vm] * 4 + [hbm] * 5,
        out_specs=(vm,) * 3,
        scratch_shapes=[
            pltpu.VMEM((3 * WIDTH, WIDTH), bf),
            pltpu.VMEM((total, WIDTH), bf),
            pltpu.SemaphoreType.DMA((5,)),
            pltpu.VMEM((total, 128), bf),
            pltpu.VMEM((16, WIDTH), f32),
            pltpu.VMEM((total, 2 * WIDTH), f32),
            pltpu.VMEM((total, 3 * WIDTH), bf),
            pltpu.VMEM((total, WIDTH), f32),
            pltpu.VMEM((total, 2 * WIDTH), f32),
            pltpu.VMEM((2, total, WIDTH), f32),
            pltpu.VMEM((2, total, 1), f32),
            pltpu.VMEM((total, 2 * WIDTH), bf),
            pltpu.VMEM((total, 2 * WIDTH), bf),
        ],
        compiler_params=pltpu.CompilerParams(vmem_limit_bytes=VMEM_LIMIT),
        name="encoder",
    )(ids, x, wc, par, tail, cot, *parts)


def prep_weights(conv1_weight):
    w1 = conv1_weight.astype(f32)
    wc = w1 - jnp.mean(w1, axis=1, keepdims=True)
    z5 = jnp.zeros((5, WIDTH), f32)
    z10 = jnp.zeros((10, WIDTH), f32)
    both = jnp.concatenate([jnp.concatenate([wc, z10], 0), jnp.concatenate([z5, wc, z5], 0)], 1)
    hi = lax.reduce_precision(both, 8, 7)
    mid = lax.reduce_precision(both - hi, 8, 7)
    low = both - hi - mid
    return jnp.concatenate([hi.astype(bf), mid.astype(bf), low.astype(bf), jnp.zeros((4, 2 * WIDTH), bf)], 0)


Y, Z, C, X = 4, 8, 2, 4
AXES = ("y", "z", "c", "x")


def flip(value, axis, size, k):
    return lax.ppermute(value, axis, [(i, i ^ k) for i in range(size)])


def turn(value, axis, size, k):
    return lax.ppermute(value, axis, [(i, (i + k) % size) for i in range(size)])


def exchange(chunks, axes):
    return lax.all_to_all(chunks, axes, 0, 0, tiled=True)


def pack(waveform, lengths):
    count = waveform.shape[0]
    at = lax.broadcasted_iota(jnp.int32, (count, SAMPLES + 128), 1)
    end = lengths[:, None]
    wide = jnp.pad(waveform, ((0, 0), (0, 128)))
    code = jnp.where(at == SAMPLES, end >> 7, jnp.where(at == SAMPLES + 1, end & 127, 0)).astype(bf)
    return jnp.where(at < SAMPLES, jnp.where(at < end, wide, jnp.zeros_like(wide)), code)


def reduce_grads(keep, send, core, shadow):
    chunks = (keep + flip(send, "c", C, 1).astype(f32)).astype(bf)
    total = jnp.sum(exchange(chunks, ("y", "x")).astype(f32), axis=0).astype(bf)
    total, shadow = lax.optimization_barrier((total, shadow))
    total = (total.astype(f32) + flip(total, "z", Z, 1).astype(f32)).astype(bf)
    a, b, c = (turn(total, "z", Z, k).astype(f32) for k in (2, 4, 6))
    total = ((total.astype(f32) + b) + (a + c)).astype(bf)
    quarters = jnp.stack([total] + [flip(total, "y", Y, k) for k in (1, 2, 3)])
    y = lax.axis_index("y")
    every = jnp.concatenate([lax.dynamic_slice_in_dim(quarters, y ^ q, 1, 0) for q in range(Y)], 0)
    half = every[:, :PART].reshape(-1, HALF)
    other = flip(half, "c", C, 1)
    grad_conv2 = jnp.where(core == 0, jnp.concatenate([half, other], 1), jnp.concatenate([other, half], 1))
    small = jnp.concatenate([every[q, PART:PART + 14, :128] for q in range(Y)], 1)
    return grad_conv2.astype(f32), small.astype(f32), shadow


def body(waveform, lengths, source, frame_mask, cotangent, conv1_weight, gain_one, shift_one,
         conv2_weight, gain_two, shift_two):
    count, frames = frame_mask.shape
    core, x = lax.axis_index("c"), lax.axis_index("x")
    own = pack(waveform, lengths)
    column = exchange(jnp.broadcast_to(own[None], (Y * Z,) + own.shape), ("y", "z"))
    parts = [conv2_weight] + [flip(conv2_weight, "x", X, k) for k in (1, 2, 3)]
    masked = cotangent * frame_mask[:, :, None].astype(bf)
    upstream = jnp.pad(masked, ((0, 0), (0, 1), (0, 0))).reshape(count * ROWS, WIDTH)
    par = jnp.concatenate(
        [jnp.stack([gain_one, shift_one, gain_two, shift_two]), jnp.zeros((4, WIDTH), f32)], 0)
    wc = prep_weights(conv1_weight)
    ids = jnp.stack([core, x])
    column, parts, upstream, par, wc, ids = lax.optimization_barrier((column, parts, upstream, par, wc, ids))
    routed = pick(ids, source, column, flip(column, "c", C, 1))
    blocks = routed[:, :SAMPLES].reshape(count * ROWS, 10)
    feat, keep, send = encoder(ids, blocks, wc, par, routed, upstream, parts)
    features = feat.reshape(count, ROWS, WIDTH)[:, :frames]
    grad_conv2, grad_front, features = reduce_grads(keep, send, core, features)
    return features, grad_conv2, grad_front


def solution(mesh):
    grid = Mesh(mesh.devices.reshape(Y, Z, C, X), AXES)
    both = P(AXES)
    placed = (both, both, both, both, both, P(), P(), P(), P("x"), P(), P())
    return jax.shard_map(
        body,
        mesh=grid,
        in_specs=placed,
        out_specs=(both, P("x"), P()),
        check_vma=False,
    )
```

```python
import math

import jax
import jax.numpy as jnp
from jax import lax
from jax.experimental import pallas as pl
from jax.experimental.pallas import tpu as pltpu
from jax.sharding import Mesh
from jax.sharding import PartitionSpec as P

f32 = jnp.float32
bf = jnp.bfloat16
WIDTH = 512
HALF = 256
ROWS = 640
SAMPLES = 6400
LOSS_SCALE = 1.0 / math.sqrt(512 * 639)
PART = 96
STRIP = 192
STEP = 64
SLOTS = PART + 16
VMEM_LIMIT = 42 * 1024 * 1024
M1, TA, TB, TC = 256, 256, 256, 320
SA, SB, SC = 64, 128, 160
NN = (((1,), (0,)), ((), ()))
NT = (((1,), (1,)), ((), ()))
TN = (((0,), (0,)), ((), ()))


def gelu_parts(y):
    d = 1.0 + 0.23164189 * jnp.abs(y)
    t = pl.reciprocal(d, approx=True)
    t = t * (2.0 - d * t)
    e = jnp.exp2(y * (y * (-0.5 * 1.4426950408889634)))
    poly = t * (0.127414796 + t * (-0.142248368 + t * (0.7107068705 + t * (-0.7265760135 + t * 0.5307027145))))
    tail = poly * e
    return jnp.where(y >= 0, 1.0 - tail, tail), e


def lane_sum(v):
    return jnp.sum(v, axis=-1, keepdims=True)


def rows8(v):
    return jnp.sum(v.reshape(v.shape[0] // 8, 8, v.shape[1]), axis=0)


def dot(a, b, dims=NN):
    return lax.dot_general(a, b, dims, preferred_element_type=f32)


def shifted_up(v, below):
    return jnp.concatenate([v, below], 0)[1:v.shape[0] + 1]


def shifted_down(v, above):
    return jnp.concatenate([above, v], 0)[7:v.shape[0] + 7]


def norm_back(q, n, inv):
    qn = q * n
    inner = lane_sum(q) * (1.0 / WIDTH)
    along = lane_sum(qn) * (1.0 / WIDTH)
    return inv * (q - inner - n * along), qn


def encoder_kernel(ids_ref, source_ref, wc_ref, par_ref, own_hbm, other_hbm, cot_hbm, mine_hbm, theirs_hbm,
                   feat_ref, keep_ref, send_ref,
                   slab_ref, slab_sems, w2_ref, cot_ref, sems, p_ref, small_ref, c_ref, u_ref, s_ref, d_ref, sg_ref, r1_ref, dl_ref, t_ref):
    total = cot_hbm.shape[0]
    core = ids_ref[0]
    for i in range(2):
        holder = source_ref[i] >> 3
        local = (holder & 1) == core

        @pl.when(local)
        def _():
            pltpu.make_async_copy(own_hbm.at[holder >> 1], slab_ref.at[i], slab_sems.at[i]).start()

        @pl.when(jnp.logical_not(local))
        def _():
            pltpu.make_async_copy(other_hbm.at[holder >> 1], slab_ref.at[i], slab_sems.at[i]).start()
    loads = []
    for n, (src, half) in enumerate(((mine_hbm, core), (theirs_hbm, 1 - core))):
        for k in range(4):
            at = pl.multiple_of((ids_ref[1] ^ k) * 2 * STRIP + half * STRIP, STRIP)
            loads.append(pltpu.make_async_copy(
                src.at[k * STRIP:(k + 1) * STRIP, :], w2_ref.at[pl.ds(at, STRIP), :], sems.at[4 * n + k]))
    loads.append(pltpu.make_async_copy(cot_hbm, cot_ref, sems.at[8]))
    for load in loads:
        load.start()
    gain1, shift1, gain2, shift2 = (par_ref[k:k + 1, :] for k in range(4))
    zero = jnp.zeros((8, WIDTH), f32)
    lengths = []

    def rows(i, size):
        return pl.ds(pl.multiple_of(i * size, size), size)

    span = 10 * STEP + 128
    tap = lax.broadcasted_iota(jnp.int32, (16, span), 0)
    at = lax.broadcasted_iota(jnp.int32, (16, span), 1)
    keep_tap = at - jnp.floor((at.astype(f32) + 0.5) * 0.1).astype(jnp.int32) * 10 == tap
    lane = lax.broadcasted_iota(jnp.int32, (span, 256), 1)
    first = ((lane & (STEP - 1)) + (lane >> 7)) * 10
    source_at = lax.broadcasted_iota(jnp.int32, (span, 256), 0)
    move = jnp.where((source_at >= first) & (source_at < first + 10), 1.0, 0.0).astype(bf)
    spread = []
    for i in range(2):
        pltpu.make_async_copy(own_hbm.at[0], slab_ref.at[i], slab_sems.at[i]).wait()
        both = slab_ref[i].astype(f32)
        crop = jnp.where((source_ref[i] & 1) == 0, both[0:1], both[1:2])
        lengths.append(crop[:, SAMPLES:SAMPLES + 1] * 128.0 + crop[:, SAMPLES + 1:SAMPLES + 2])
        for g in range(10):
            part = crop[:, g * 10 * STEP:g * 10 * STEP + span]
            spread.append(jnp.where(keep_tap, part, 0.0).astype(bf))
    moved = dot(jnp.concatenate(spread, 0), move)
    left = lax.broadcasted_iota(jnp.int32, (16, 128), 1) < STEP
    for g in range(10):
        for n in range(2):
            lanes = slice(128 * n, 128 * (n + 1))
            pair = jnp.where(left, moved[32 * g:32 * g + 16, lanes], moved[32 * g + 16:32 * g + 32, lanes]).astype(bf)
            for copy in range(3):
                p_ref[32 * copy + 16 * n:32 * copy + 16 * (n + 1), 128 * g:128 * (g + 1)] = pair

    def conv1(i, _):
        r = rows(i, M1)
        c_ref[r, :] = dot(p_ref[:, r], wc_ref[...], TN)
        return 0
    lax.fori_loop(0, total // M1, conv1, 0)

    def level_one(t, below):
        for j in reversed(range(TA // SA)):
            below = level_one_rows(pl.ds(pl.multiple_of(t * TA + j * SA, SA), SA), below)
        return below

    def level_one_rows(r, below):
        for half in range(2):
            c = c_ref[r, half * WIDTH:(half + 1) * WIDTH]
            inv = lax.rsqrt(lane_sum(c * c) * (1.0 / WIDTH) + 1e-5)
            y = c * inv * gain1 + shift1
            phi, e = gelu_parts(y)
            h = y * phi
            sg_ref[half, r, :] = (phi + (y * 0.3989422804014327) * e) * gain1
            r1_ref[half, r, :] = inv
            u_ref[r, half * WIDTH:(half + 1) * WIDTH] = h.astype(bf)
            if half == 0:
                u_ref[r, 2 * WIDTH:] = shifted_up(h, below).astype(bf)
                first = h[0:8]
        return first

    def conv2(t):
        r = rows(t, TA)
        s_ref[r, :] = dot(u_ref[r, :], w2_ref[...])

    def forward(i, below):
        t = total // TA - 2 - i
        conv2(t + 1)
        return level_one(t, below)
    below = level_one(total // TA - 1, zero)
    for load in loads[:8]:
        load.wait()
    lax.fori_loop(0, total // TA - 1, forward, below)
    conv2(0)

    loads[8].wait()

    def level_two(t, carry):
        for j in range(TB // SB):
            carry = level_two_rows(pl.multiple_of(t * TB + j * SB, SB), carry)
        return carry

    def level_two_rows(b, carry):
        acc_a, acc_b, above = carry
        r = pl.ds(b, SB)
        z = s_ref[r, :]
        c = z - lane_sum(z) * (1.0 / WIDTH)
        inv = lax.rsqrt(lane_sum(c * c) * (1.0 / WIDTH) + 1e-5)
        n = c * inv
        y = n * gain2 + shift2
        phi, e = gelu_parts(y)
        feat_ref[r, :] = (y * phi).astype(bf)
        slope = phi + (y * 0.3989422804014327) * e
        row = (lax.broadcasted_iota(jnp.int32, (SB, 1), 0) + b).astype(f32)
        room = jnp.where(row < ROWS, lengths[0], lengths[1] + 10.0 * ROWS)
        weight = jnp.where(10.0 * row + 19.0 < room, LOSS_SCALE, 0.0)
        q = cot_ref[r, :].astype(f32) * weight * (slope * gain2)
        back, qn = norm_back(q, n, inv)
        dl_ref[r, 0:WIDTH] = back.astype(bf)
        dl_ref[r, WIDTH:] = shifted_down(back, above).astype(bf)
        return acc_a + rows8(qn), acc_b + rows8(q), back[SB - 8:SB]

    def down(t):
        r = rows(t, TB)
        now = dl_ref[r, 0:WIDTH]
        d_ref[r, 0:WIDTH] = dot(now, w2_ref[0:WIDTH, :], NT) + dot(dl_ref[r, WIDTH:], w2_ref[2 * WIDTH:, :], NT)
        d_ref[r, WIDTH:] = dot(now, w2_ref[WIDTH:2 * WIDTH, :], NT)

    def middle(t, carry):
        down(t - 1)
        return level_two(t, carry)
    carry = level_two(0, (zero, zero, zero))
    acc_a, acc_b, _ = lax.fori_loop(1, total // TB, middle, carry)
    down(total // TB - 1)
    small_ref[12:13, :] = jnp.sum(acc_a, axis=0, keepdims=True) / gain2
    small_ref[13:14, :] = jnp.sum(acc_b, axis=0, keepdims=True) / gain2
    small_ref[14:16, :] = jnp.zeros((2, WIDTH), f32)

    def level_one_back(r, acc_a, acc_b):
        for half in range(2):
            lanes = slice(half * WIDTH, (half + 1) * WIDTH)
            q = d_ref[r, lanes] * sg_ref[half, r, :]
            inv = r1_ref[half, r, :]
            back, qn = norm_back(q, c_ref[r, lanes] * inv, inv)
            t_ref[r, lanes] = back.astype(bf)
            acc_a = acc_a + rows8(qn)
            acc_b = acc_b + rows8(q)
        return acc_a, acc_b

    def backward(i, acc):
        acc_a, acc_b = acc
        chunk = 3 * WIDTH // (total // TC)
        for ref, half in ((keep_ref, core), (send_ref, 1 - core)):
            cols = pl.ds(pl.multiple_of(half * HALF, HALF), HALF)
            grad = dot(u_ref[:, pl.ds(pl.multiple_of(i * chunk, chunk), chunk)], dl_ref[:, cols], TN).astype(ref.dtype)
            for j in range(4):
                ref[4 * j + i, 0:PART, :] = grad[j * PART:(j + 1) * PART]
        for j in range(TC // SC):
            acc_a, acc_b = level_one_back(pl.ds(pl.multiple_of(i * TC + j * SC, SC), SC), acc_a, acc_b)
        return acc_a, acc_b
    acc_a, acc_b = lax.fori_loop(0, total // TC, backward, (zero, zero))
    small_ref[10:11, :] = jnp.sum(acc_a, axis=0, keepdims=True) / gain1
    small_ref[11:12, :] = jnp.sum(acc_b, axis=0, keepdims=True) / gain1
    taps = dot(p_ref[0:32, :], t_ref[...])
    odd = jnp.concatenate([taps[5:10, WIDTH:], taps[16:21, WIDTH:]], 0)
    small_ref[0:10, :] = taps[0:10, 0:WIDTH] + odd
    small = small_ref[...].astype(bf)
    for j in range(4):
        quarter = jnp.concatenate([small[:, 128 * j:128 * (j + 1)], jnp.zeros((16, 128), bf)], 1)
        for i in range(4):
            send_ref[4 * j + i, PART:SLOTS, :] = quarter
            keep_ref[4 * j + i, PART:SLOTS, :] = quarter.astype(f32)


def encoder(ids, source, wc, par, own, other, cot, mine, theirs):
    total = cot.shape[0]
    vm = pl.BlockSpec(memory_space=pltpu.VMEM)
    hbm = pl.BlockSpec(memory_space=pl.ANY)
    return pl.pallas_call(
        encoder_kernel,
        out_shape=(
            jax.ShapeDtypeStruct((total, WIDTH), bf),
            jax.ShapeDtypeStruct((16, SLOTS, HALF), f32),
            jax.ShapeDtypeStruct((16, SLOTS, HALF), bf),
        ),
        in_specs=[pl.BlockSpec(memory_space=pltpu.SMEM)] * 2 + [vm] * 2 + [hbm] * 5,
        out_specs=(vm,) * 3,
        scratch_shapes=[
            pltpu.VMEM((2,) + own.shape[1:], bf),
            pltpu.SemaphoreType.DMA((2,)),
            pltpu.VMEM((3 * WIDTH, WIDTH), bf),
            pltpu.VMEM((total, WIDTH), bf),
            pltpu.SemaphoreType.DMA((9,)),
            pltpu.VMEM((96, total), bf),
            pltpu.VMEM((16, WIDTH), f32),
            pltpu.VMEM((total, 2 * WIDTH), f32),
            pltpu.VMEM((total, 3 * WIDTH), bf),
            pltpu.VMEM((total, WIDTH), f32),
            pltpu.VMEM((total, 2 * WIDTH), f32),
            pltpu.VMEM((2, total, WIDTH), f32),
            pltpu.VMEM((2, total, 1), f32),
            pltpu.VMEM((total, 2 * WIDTH), bf),
            pltpu.VMEM((total, 2 * WIDTH), bf),
        ],
        compiler_params=pltpu.CompilerParams(vmem_limit_bytes=VMEM_LIMIT),
        name="encoder",
    )(ids, source, wc, par, own, other, cot, mine, theirs)


def prep_weights(conv1_weight):
    w1 = conv1_weight.astype(f32)
    wc = w1 - jnp.mean(w1, axis=1, keepdims=True)
    even = jnp.pad(wc, ((0, 22), (0, 0)))
    odd = jnp.pad(jnp.concatenate([wc[:5], jnp.zeros((6, WIDTH), f32), wc[5:]], 0), ((5, 11), (0, 0)))
    both = jnp.concatenate([even, odd], 1)
    hi = lax.reduce_precision(both, 8, 7)
    mid = lax.reduce_precision(both - hi, 8, 7)
    low = both - hi - mid
    return jnp.concatenate([hi.astype(bf), mid.astype(bf), low.astype(bf)], 0)


def pack_kernel(lengths_ref, wave_ref, out_ref):
    row = lax.broadcasted_iota(jnp.int32, (2, SAMPLES), 0)
    at = lax.broadcasted_iota(jnp.int32, (2, SAMPLES), 1)
    end = jnp.where(row == 0, lengths_ref[0], lengths_ref[1])
    cleaned = jnp.where(at < end, wave_ref[...].astype(f32), 0.0)
    lane, last = at[:, :128], end[:, :128]
    code = jnp.where(lane == 0, last >> 7, jnp.where(lane == 1, last & 127, 0)).astype(f32)
    block = jnp.concatenate([cleaned, code], 1).astype(bf)
    for k in range(out_ref.shape[0]):
        out_ref[k] = block


def pack(waveform, lengths, copies):
    return pl.pallas_call(
        pack_kernel,
        out_shape=jax.ShapeDtypeStruct((copies, 2, SAMPLES + 128), bf),
        in_specs=[pl.BlockSpec(memory_space=pltpu.SMEM), pl.BlockSpec(memory_space=pltpu.VMEM)],
        out_specs=pl.BlockSpec(memory_space=pltpu.VMEM),
        name="pack",
    )(lengths, waveform)


Y, Z, C, X = 4, 8, 2, 4
AXES = ("y", "z", "c", "x")


def flip(value, axis, size, k):
    return lax.ppermute(value, axis, [(i, i ^ k) for i in range(size)])


def turn(value, axis, size, k):
    return lax.ppermute(value, axis, [(i, (i + k) % size) for i in range(size)])


def exchange(chunks, axes):
    return lax.all_to_all(chunks, axes, 0, 0, tiled=True)


def reduce_grads(keep, send, core, shadow):
    chunks = (keep + flip(send, "c", C, 1).astype(f32)).astype(bf)
    total = jnp.sum(exchange(chunks, ("y", "x")).astype(f32), axis=0).astype(bf)
    total, shadow = lax.optimization_barrier((total, shadow))
    a, b, c = (turn(total, "z", Z, k).astype(f32) for k in (2, 4, 6))
    total = ((total.astype(f32) + b) + (a + c)).astype(bf)
    total = (total.astype(f32) + flip(total, "z", Z, 1).astype(f32)).astype(bf)
    quarters = jnp.stack([total] + [flip(total, "y", Y, k) for k in (1, 2, 3)])
    y = lax.axis_index("y")
    every = jnp.concatenate([lax.dynamic_slice_in_dim(quarters, y ^ q, 1, 0) for q in range(Y)], 0)
    half = every[:, :PART].reshape(-1, HALF)
    other = flip(half, "c", C, 1)
    grad_conv2 = jnp.where(core == 0, jnp.concatenate([half, other], 1), jnp.concatenate([other, half], 1))
    small = jnp.concatenate([every[q, PART:PART + 14, :128] for q in range(Y)], 1)
    return grad_conv2.astype(f32), small.astype(f32), shadow


def body(waveform, lengths, source, frame_mask, cotangent, conv1_weight, gain_one, shift_one,
         conv2_weight, gain_two, shift_two):
    count, frames = frame_mask.shape
    core, x = lax.axis_index("c"), lax.axis_index("x")
    column = exchange(pack(waveform, lengths, Y * Z), ("y", "z"))
    strip = lax.dynamic_slice_in_dim(conv2_weight, core * STRIP, STRIP, 0)
    pair = jnp.concatenate([strip, flip(strip, "x", X, 1)], 0)
    mine = jnp.concatenate([pair, flip(pair, "x", X, 2)], 0)
    theirs = flip(mine, "c", C, 1)
    masked = cotangent * frame_mask[:, :, None].astype(bf)
    upstream = jnp.pad(masked, ((0, 0), (0, 1), (0, 0))).reshape(count * ROWS, WIDTH)
    par = jnp.concatenate(
        [jnp.stack([gain_one, shift_one, gain_two, shift_two]), jnp.zeros((4, WIDTH), f32)], 0)
    wc = prep_weights(conv1_weight)
    ids = jnp.stack([core, x])
    column, mine, theirs, upstream, par, wc, ids = lax.optimization_barrier(
        (column, mine, theirs, upstream, par, wc, ids))
    feat, keep, send = encoder(ids, source, wc, par, column, flip(column, "c", C, 1), upstream, mine, theirs)
    features = feat.reshape(count, ROWS, WIDTH)[:, :frames]
    grad_conv2, grad_front, features = reduce_grads(keep, send, core, features)
    return features, grad_conv2, grad_front


def solution(mesh):
    grid = Mesh(mesh.devices.reshape(Y, Z, C, X), AXES)
    both = P(AXES)
    placed = (both, both, both, both, both, P(), P(), P(), P("x"), P(), P())
    return jax.shard_map(
        body,
        mesh=grid,
        in_specs=placed,
        out_specs=(both, P("x"), P()),
        check_vma=False,
    )
```

```python
import math

import jax
import jax.numpy as jnp
from jax import lax
from jax.experimental import pallas as pl
from jax.experimental.pallas import tpu as pltpu
from jax.sharding import Mesh
from jax.sharding import PartitionSpec as P

f32 = jnp.float32
bf = jnp.bfloat16
WIDTH = 512
HALF = 256
ROWS = 640
SAMPLES = 6400
LOSS_SCALE = 1.0 / math.sqrt(512 * 639)
PART = 96
STRIP = 192
BLOCK = 384
STEP = 64
SLOTS = PART + 16
VMEM_LIMIT = 42 * 1024 * 1024
M1, TA, TB, TC = 256, 640, 640, 640
SA, SB, SC = 64, 320, 320
NN = (((1,), (0,)), ((), ()))
NT = (((1,), (1,)), ((), ()))
TN = (((0,), (0,)), ((), ()))


def gelu_parts(y):
    d = 1.0 + 0.23164189 * jnp.abs(y)
    t = pl.reciprocal(d, approx=True)
    t = t * (2.0 - d * t)
    e = jnp.exp2(y * (y * (-0.5 * 1.4426950408889634)))
    poly = t * (0.127414796 + t * (-0.142248368 + t * (0.7107068705 + t * (-0.7265760135 + t * 0.5307027145))))
    tail = poly * e
    return jnp.where(y >= 0, 1.0 - tail, tail), e


def lane_sum(v):
    return jnp.sum(v, axis=-1, keepdims=True)


def rows8(v):
    return jnp.sum(v.reshape(v.shape[0] // 8, 8, v.shape[1]), axis=0)


def dot(a, b, dims=NN):
    return lax.dot_general(a, b, dims, preferred_element_type=f32)


def shifted_up(v, below):
    return jnp.concatenate([v, below], 0)[1:v.shape[0] + 1]


def shifted_down(v, above):
    return jnp.concatenate([above, v], 0)[7:v.shape[0] + 7]


def norm_back(q, n, inv):
    qn = q * n
    inner = lane_sum(q) * (1.0 / WIDTH)
    along = lane_sum(qn) * (1.0 / WIDTH)
    return inv * (q - inner - n * along), qn


def encoder_kernel(ids_ref, source_ref, wc_ref, par_ref, own_hbm, other_hbm, cot_hbm, mine_hbm, theirs_hbm,
                   feat_ref, keep_ref, send_ref,
                   slab_ref, slab_sems, w2_ref, cot_ref, sems, p_ref, small_ref, c_ref, u_ref, s_ref, d_ref, sg_ref, r1_ref, dl_ref, t_ref):
    total = cot_hbm.shape[0]
    core = ids_ref[0]
    for i in range(2):
        holder = source_ref[i] >> 3
        local = (holder & 1) == core

        @pl.when(local)
        def _():
            pltpu.make_async_copy(own_hbm.at[holder >> 1], slab_ref.at[i], slab_sems.at[i]).start()

        @pl.when(jnp.logical_not(local))
        def _():
            pltpu.make_async_copy(other_hbm.at[holder >> 1], slab_ref.at[i], slab_sems.at[i]).start()
    loads = []
    for n, (src, half) in enumerate(((mine_hbm, core), (theirs_hbm, 1 - core))):
        for k in range(4):
            at = pl.multiple_of((ids_ref[1] ^ k) * 2 * STRIP + half * STRIP, STRIP)
            loads.append(pltpu.make_async_copy(
                src.at[k * STRIP:(k + 1) * STRIP, :], w2_ref.at[pl.ds(at, STRIP), :], sems.at[4 * n + k]))
    loads.append(pltpu.make_async_copy(cot_hbm, cot_ref, sems.at[8]))
    for load in loads:
        load.start()
    gain1, shift1, gain2, shift2 = (par_ref[k:k + 1, :] for k in range(4))
    zero = jnp.zeros((8, WIDTH), f32)
    lengths = []

    def rows(i, size):
        return pl.ds(pl.multiple_of(i * size, size), size)

    span = 10 * STEP + 128
    tap = lax.broadcasted_iota(jnp.int32, (16, span), 0)
    at = lax.broadcasted_iota(jnp.int32, (16, span), 1)
    keep_tap = at - jnp.floor((at.astype(f32) + 0.5) * 0.1).astype(jnp.int32) * 10 == tap
    lane = lax.broadcasted_iota(jnp.int32, (span, 256), 1)
    first = ((lane & (STEP - 1)) + (lane >> 7)) * 10
    source_at = lax.broadcasted_iota(jnp.int32, (span, 256), 0)
    move = jnp.where((source_at >= first) & (source_at < first + 10), 1.0, 0.0).astype(bf)
    spread = []
    for i in range(2):
        pltpu.make_async_copy(own_hbm.at[0], slab_ref.at[i], slab_sems.at[i]).wait()
        both = slab_ref[i].astype(f32)
        crop = jnp.where((source_ref[i] & 1) == 0, both[0:1], both[1:2])
        lengths.append(crop[:, SAMPLES:SAMPLES + 1] * 128.0 + crop[:, SAMPLES + 1:SAMPLES + 2])
        for g in range(10):
            part = crop[:, g * 10 * STEP:g * 10 * STEP + span]
            spread.append(jnp.where(keep_tap, part, 0.0).astype(bf))
    moved = dot(jnp.concatenate(spread, 0), move)
    left = lax.broadcasted_iota(jnp.int32, (16, 128), 1) < STEP
    for g in range(10):
        for n in range(2):
            lanes = slice(128 * n, 128 * (n + 1))
            pair = jnp.where(left, moved[32 * g:32 * g + 16, lanes], moved[32 * g + 16:32 * g + 32, lanes]).astype(bf)
            for copy in range(3):
                p_ref[32 * copy + 16 * n:32 * copy + 16 * (n + 1), 128 * g:128 * (g + 1)] = pair

    def conv1(i, _):
        r = rows(i, M1)
        c_ref[r, :] = dot(p_ref[:, r], wc_ref[...], TN)
        return 0
    lax.fori_loop(0, total // M1, conv1, 0)

    def level_one(t, below):
        for j in reversed(range(TA // SA)):
            below = level_one_rows(pl.ds(pl.multiple_of(t * TA + j * SA, SA), SA), below)
        return below

    def level_one_rows(r, below):
        for half in range(2):
            c = c_ref[r, half * WIDTH:(half + 1) * WIDTH]
            inv = lax.rsqrt(lane_sum(c * c) * (1.0 / WIDTH) + 1e-5)
            y = c * inv * gain1 + shift1
            phi, e = gelu_parts(y)
            h = y * phi
            sg_ref[half, r, :] = (phi + (y * 0.3989422804014327) * e) * gain1
            r1_ref[half, r, :] = inv
            u_ref[r, half * WIDTH:(half + 1) * WIDTH] = h.astype(bf)
            if half == 0:
                u_ref[r, 2 * WIDTH:] = shifted_up(h, below).astype(bf)
                first = h[0:8]
        return first

    def conv2(t):
        r = rows(t, TA)
        s_ref[r, :] = dot(u_ref[r, :], w2_ref[...])

    def forward(i, below):
        t = total // TA - 2 - i
        conv2(t + 1)
        return level_one(t, below)
    below = level_one(total // TA - 1, zero)
    for load in loads[:8]:
        load.wait()
    lax.fori_loop(0, total // TA - 1, forward, below)
    conv2(0)

    loads[8].wait()

    def level_two(t, carry):
        for j in range(TB // SB):
            carry = level_two_rows(pl.multiple_of(t * TB + j * SB, SB), carry)
        return carry

    def level_two_rows(b, carry):
        acc_a, acc_b, above = carry
        r = pl.ds(b, SB)
        z = s_ref[r, :]
        c = z - lane_sum(z) * (1.0 / WIDTH)
        inv = lax.rsqrt(lane_sum(c * c) * (1.0 / WIDTH) + 1e-5)
        n = c * inv
        y = n * gain2 + shift2
        phi, e = gelu_parts(y)
        feat_ref[r, :] = (y * phi).astype(bf)
        slope = phi + (y * 0.3989422804014327) * e
        row = (lax.broadcasted_iota(jnp.int32, (SB, 1), 0) + b).astype(f32)
        room = jnp.where(row < ROWS, lengths[0], lengths[1] + 10.0 * ROWS)
        weight = jnp.where(10.0 * row + 19.0 < room, LOSS_SCALE, 0.0)
        q = cot_ref[r, :].astype(f32) * weight * (slope * gain2)
        back, qn = norm_back(q, n, inv)
        dl_ref[r, 0:WIDTH] = back.astype(bf)
        dl_ref[r, WIDTH:] = shifted_down(back, above).astype(bf)
        return acc_a + rows8(qn), acc_b + rows8(q), back[SB - 8:SB]

    def down(t):
        r = rows(t, TB)
        now = dl_ref[r, 0:WIDTH]
        d_ref[r, 0:WIDTH] = dot(now, w2_ref[0:WIDTH, :], NT) + dot(dl_ref[r, WIDTH:], w2_ref[2 * WIDTH:, :], NT)
        d_ref[r, WIDTH:] = dot(now, w2_ref[WIDTH:2 * WIDTH, :], NT)

    def middle(t, carry):
        down(t - 1)
        return level_two(t, carry)
    carry = level_two(0, (zero, zero, zero))
    acc_a, acc_b, _ = lax.fori_loop(1, total // TB, middle, carry)
    down(total // TB - 1)
    small_ref[12:13, :] = jnp.sum(acc_a, axis=0, keepdims=True) / gain2
    small_ref[13:14, :] = jnp.sum(acc_b, axis=0, keepdims=True) / gain2
    small_ref[14:16, :] = jnp.zeros((2, WIDTH), f32)

    def level_one_back(r, acc_a, acc_b):
        for half in range(2):
            lanes = slice(half * WIDTH, (half + 1) * WIDTH)
            q = d_ref[r, lanes] * sg_ref[half, r, :]
            inv = r1_ref[half, r, :]
            back, qn = norm_back(q, c_ref[r, lanes] * inv, inv)
            t_ref[r, lanes] = back.astype(bf)
            acc_a = acc_a + rows8(qn)
            acc_b = acc_b + rows8(q)
        return acc_a, acc_b

    def backward(i, acc):
        acc_a, acc_b = acc
        chunk = 3 * WIDTH // (total // TC)
        for ref, half in ((keep_ref, core), (send_ref, 1 - core)):
            cols = pl.ds(pl.multiple_of(half * HALF, HALF), HALF)
            grad = dot(u_ref[:, pl.ds(pl.multiple_of(i * chunk, chunk), chunk)], dl_ref[:, cols], TN).astype(ref.dtype)
            blocks = chunk // BLOCK
            for b in range(blocks):
                for j in range(4):
                    start = b * BLOCK + j * PART
                    ref[4 * j + blocks * i + b, 0:PART, :] = grad[start:start + PART]
        for j in range(TC // SC):
            acc_a, acc_b = level_one_back(pl.ds(pl.multiple_of(i * TC + j * SC, SC), SC), acc_a, acc_b)
        return acc_a, acc_b
    acc_a, acc_b = lax.fori_loop(0, total // TC, backward, (zero, zero))
    small_ref[10:11, :] = jnp.sum(acc_a, axis=0, keepdims=True) / gain1
    small_ref[11:12, :] = jnp.sum(acc_b, axis=0, keepdims=True) / gain1
    taps = dot(p_ref[0:32, :], t_ref[...])
    odd = jnp.concatenate([taps[5:10, WIDTH:], taps[16:21, WIDTH:]], 0)
    small_ref[0:10, :] = taps[0:10, 0:WIDTH] + odd
    small = small_ref[...].astype(bf)
    for j in range(4):
        quarter = jnp.concatenate([small[:, 128 * j:128 * (j + 1)], jnp.zeros((16, 128), bf)], 1)
        for i in range(4):
            send_ref[4 * j + i, PART:SLOTS, :] = quarter
            keep_ref[4 * j + i, PART:SLOTS, :] = quarter.astype(f32)


def encoder(ids, source, wc, par, own, other, cot, mine, theirs):
    total = cot.shape[0]
    vm = pl.BlockSpec(memory_space=pltpu.VMEM)
    hbm = pl.BlockSpec(memory_space=pl.ANY)
    return pl.pallas_call(
        encoder_kernel,
        out_shape=(
            jax.ShapeDtypeStruct((total, WIDTH), bf),
            jax.ShapeDtypeStruct((16, SLOTS, HALF), f32),
            jax.ShapeDtypeStruct((16, SLOTS, HALF), bf),
        ),
        in_specs=[pl.BlockSpec(memory_space=pltpu.SMEM)] * 2 + [vm] * 2 + [hbm] * 5,
        out_specs=(vm,) * 3,
        scratch_shapes=[
            pltpu.VMEM((2,) + own.shape[1:], bf),
            pltpu.SemaphoreType.DMA((2,)),
            pltpu.VMEM((3 * WIDTH, WIDTH), bf),
            pltpu.VMEM((total, WIDTH), bf),
            pltpu.SemaphoreType.DMA((9,)),
            pltpu.VMEM((96, total), bf),
            pltpu.VMEM((16, WIDTH), f32),
            pltpu.VMEM((total, 2 * WIDTH), f32),
            pltpu.VMEM((total, 3 * WIDTH), bf),
            pltpu.VMEM((total, WIDTH), f32),
            pltpu.VMEM((total, 2 * WIDTH), f32),
            pltpu.VMEM((2, total, WIDTH), f32),
            pltpu.VMEM((2, total, 1), f32),
            pltpu.VMEM((total, 2 * WIDTH), bf),
            pltpu.VMEM((total, 2 * WIDTH), bf),
        ],
        compiler_params=pltpu.CompilerParams(vmem_limit_bytes=VMEM_LIMIT),
        name="encoder",
    )(ids, source, wc, par, own, other, cot, mine, theirs)


def prep_weights(conv1_weight):
    w1 = conv1_weight.astype(f32)
    wc = w1 - jnp.mean(w1, axis=1, keepdims=True)
    even = jnp.pad(wc, ((0, 22), (0, 0)))
    odd = jnp.pad(jnp.concatenate([wc[:5], jnp.zeros((6, WIDTH), f32), wc[5:]], 0), ((5, 11), (0, 0)))
    both = jnp.concatenate([even, odd], 1)
    hi = lax.reduce_precision(both, 8, 7)
    mid = lax.reduce_precision(both - hi, 8, 7)
    low = both - hi - mid
    return jnp.concatenate([hi.astype(bf), mid.astype(bf), low.astype(bf)], 0)


def pack_kernel(lengths_ref, wave_ref, out_ref):
    row = lax.broadcasted_iota(jnp.int32, (2, SAMPLES), 0)
    at = lax.broadcasted_iota(jnp.int32, (2, SAMPLES), 1)
    end = jnp.where(row == 0, lengths_ref[0], lengths_ref[1])
    cleaned = jnp.where(at < end, wave_ref[...].astype(f32), 0.0)
    lane, last = at[:, :128], end[:, :128]
    code = jnp.where(lane == 0, last >> 7, jnp.where(lane == 1, last & 127, 0)).astype(f32)
    block = jnp.concatenate([cleaned, code], 1).astype(bf)
    for k in range(out_ref.shape[0]):
        out_ref[k] = block


def pack(waveform, lengths, copies):
    return pl.pallas_call(
        pack_kernel,
        out_shape=jax.ShapeDtypeStruct((copies, 2, SAMPLES + 128), bf),
        in_specs=[pl.BlockSpec(memory_space=pltpu.SMEM), pl.BlockSpec(memory_space=pltpu.VMEM)],
        out_specs=pl.BlockSpec(memory_space=pltpu.VMEM),
        name="pack",
    )(lengths, waveform)


Y, Z, C, X = 4, 8, 2, 4
AXES = ("y", "z", "c", "x")


def flip(value, axis, size, k):
    return lax.ppermute(value, axis, [(i, i ^ k) for i in range(size)])


def turn(value, axis, size, k):
    return lax.ppermute(value, axis, [(i, (i + k) % size) for i in range(size)])


def exchange(chunks, axes):
    return lax.all_to_all(chunks, axes, 0, 0, tiled=True)


def reduce_grads(keep, send, core, shadow):
    chunks = (keep + flip(send, "c", C, 1).astype(f32)).astype(bf)
    total = jnp.sum(exchange(chunks, ("y", "x")).astype(f32), axis=0).astype(bf)
    total, shadow = lax.optimization_barrier((total, shadow))
    a, b, c = (turn(total, "z", Z, k).astype(f32) for k in (2, 4, 6))
    total = ((total.astype(f32) + b) + (a + c)).astype(bf)
    total = (total.astype(f32) + flip(total, "z", Z, 1).astype(f32)).astype(bf)
    quarters = jnp.stack([total] + [flip(total, "y", Y, k) for k in (1, 2, 3)])
    y = lax.axis_index("y")
    every = jnp.concatenate([lax.dynamic_slice_in_dim(quarters, y ^ q, 1, 0) for q in range(Y)], 0)
    half = every[:, :PART].reshape(-1, HALF)
    other = flip(half, "c", C, 1)
    grad_conv2 = jnp.where(core == 0, jnp.concatenate([half, other], 1), jnp.concatenate([other, half], 1))
    small = jnp.concatenate([every[q, PART:PART + 14, :128] for q in range(Y)], 1)
    return grad_conv2.astype(f32), small.astype(f32), shadow


def body(waveform, lengths, source, frame_mask, cotangent, conv1_weight, gain_one, shift_one,
         conv2_weight, gain_two, shift_two):
    count, frames = frame_mask.shape
    core, x = lax.axis_index("c"), lax.axis_index("x")
    column = exchange(pack(waveform, lengths, Y * Z), ("y", "z"))
    strip = lax.dynamic_slice_in_dim(conv2_weight, core * STRIP, STRIP, 0)
    pair = jnp.concatenate([strip, flip(strip, "x", X, 1)], 0)
    mine = jnp.concatenate([pair, flip(pair, "x", X, 2)], 0)
    theirs = flip(mine, "c", C, 1)
    masked = cotangent * frame_mask[:, :, None].astype(bf)
    upstream = jnp.pad(masked, ((0, 0), (0, 1), (0, 0))).reshape(count * ROWS, WIDTH)
    par = jnp.concatenate(
        [jnp.stack([gain_one, shift_one, gain_two, shift_two]), jnp.zeros((4, WIDTH), f32)], 0)
    wc = prep_weights(conv1_weight)
    ids = jnp.stack([core, x])
    column, mine, theirs, upstream, par, wc, ids = lax.optimization_barrier(
        (column, mine, theirs, upstream, par, wc, ids))
    feat, keep, send = encoder(ids, source, wc, par, column, flip(column, "c", C, 1), upstream, mine, theirs)
    features = feat.reshape(count, ROWS, WIDTH)[:, :frames]
    grad_conv2, grad_front, features = reduce_grads(keep, send, core, features)
    return features, grad_conv2, grad_front


def solution(mesh):
    grid = Mesh(mesh.devices.reshape(Y, Z, C, X), AXES)
    both = P(AXES)
    placed = (both, both, both, both, both, P(), P(), P(), P("x"), P(), P())
    return jax.shard_map(
        body,
        mesh=grid,
        in_specs=placed,
        out_specs=(both, P("x"), P()),
        check_vma=False,
    )
```

```python
import math

import jax
import jax.numpy as jnp
from jax import lax
from jax.experimental import pallas as pl
from jax.experimental.pallas import tpu as pltpu
from jax.sharding import Mesh
from jax.sharding import PartitionSpec as P

f32 = jnp.float32
bf = jnp.bfloat16
WIDTH = 512
HALF = 256
ROWS = 640
SAMPLES = 6400
LOSS_SCALE = 1.0 / math.sqrt(512 * 639)
PART = 96
STRIP = 192
BLOCK = 384
STEP = 64
SLOTS = PART + 16
VMEM_LIMIT = 52 * 1024 * 1024
M1, TA, TB, TC = 640, 640, 640, 640
SA, SB, SC = 64, 320, 320
NN = (((1,), (0,)), ((), ()))
NT = (((1,), (1,)), ((), ()))
TN = (((0,), (0,)), ((), ()))


def gelu_parts(y):
    d = 1.0 + 0.23164189 * jnp.abs(y)
    t = pl.reciprocal(d, approx=True)
    t = t * (2.0 - d * t)
    e = jnp.exp2(y * (y * (-0.5 * 1.4426950408889634)))
    poly = t * (0.127414796 + t * (-0.142248368 + t * (0.7107068705 + t * (-0.7265760135 + t * 0.5307027145))))
    tail = poly * e
    return jnp.where(y >= 0, 1.0 - tail, tail), e


def lane_sum(v):
    return jnp.sum(v, axis=-1, keepdims=True)


def rows8(v):
    return jnp.sum(v.reshape(v.shape[0] // 8, 8, v.shape[1]), axis=0)


def dot(a, b, dims=NN):
    return lax.dot_general(a, b, dims, preferred_element_type=f32)


def shifted_up(v, below):
    return jnp.concatenate([v, below], 0)[1:v.shape[0] + 1]


def shifted_down(v, above):
    return jnp.concatenate([above, v], 0)[7:v.shape[0] + 7]


def norm_back(q, n, inv):
    qn = q * n
    inner = lane_sum(q) * (1.0 / WIDTH)
    along = lane_sum(qn) * (1.0 / WIDTH)
    return inv * (q - inner - n * along), qn


def encoder_kernel(ids_ref, source_ref, wc_ref, par_ref, own_hbm, other_hbm, cot_hbm, mine_hbm, theirs_hbm,
                   feat_ref, keep_ref, send_ref,
                   slab_ref, slab_sems, w2_ref, cot_ref, sems, p_ref, small_ref, c_ref, u_ref, s_ref, d_ref, sg_ref, r1_ref, dl_ref, t_ref):
    total = cot_hbm.shape[0]
    core = ids_ref[0]
    for i in range(2):
        holder = source_ref[i] >> 3
        local = (holder & 1) == core

        @pl.when(local)
        def _():
            pltpu.make_async_copy(own_hbm.at[holder >> 1], slab_ref.at[i], slab_sems.at[i]).start()

        @pl.when(jnp.logical_not(local))
        def _():
            pltpu.make_async_copy(other_hbm.at[holder >> 1], slab_ref.at[i], slab_sems.at[i]).start()
    loads = []
    for n, (src, half) in enumerate(((mine_hbm, core), (theirs_hbm, 1 - core))):
        for k in range(4):
            at = pl.multiple_of((ids_ref[1] ^ k) * 2 * STRIP + half * STRIP, STRIP)
            loads.append(pltpu.make_async_copy(
                src.at[k * STRIP:(k + 1) * STRIP, :], w2_ref.at[pl.ds(at, STRIP), :], sems.at[4 * n + k]))
    loads.append(pltpu.make_async_copy(cot_hbm, cot_ref, sems.at[8]))
    for load in loads:
        load.start()
    gain1, shift1, gain2, shift2 = (par_ref[k:k + 1, :] for k in range(4))
    zero = jnp.zeros((8, WIDTH), f32)
    lengths = []

    def rows(i, size):
        return pl.ds(pl.multiple_of(i * size, size), size)

    span = 10 * STEP + 128
    tap = lax.broadcasted_iota(jnp.int32, (16, span), 0)
    at = lax.broadcasted_iota(jnp.int32, (16, span), 1)
    keep_tap = at - jnp.floor((at.astype(f32) + 0.5) * 0.1).astype(jnp.int32) * 10 == tap
    lane = lax.broadcasted_iota(jnp.int32, (span, 256), 1)
    first = ((lane & (STEP - 1)) + (lane >> 7)) * 10
    source_at = lax.broadcasted_iota(jnp.int32, (span, 256), 0)
    move = jnp.where((source_at >= first) & (source_at < first + 10), 1.0, 0.0).astype(bf)
    spread = []
    for i in range(2):
        pltpu.make_async_copy(own_hbm.at[0], slab_ref.at[i], slab_sems.at[i]).wait()
        both = slab_ref[i].astype(f32)
        crop = jnp.where((source_ref[i] & 1) == 0, both[0:1], both[1:2])
        lengths.append(crop[:, SAMPLES:SAMPLES + 1] * 128.0 + crop[:, SAMPLES + 1:SAMPLES + 2])
        for g in range(10):
            part = crop[:, g * 10 * STEP:g * 10 * STEP + span]
            spread.append(jnp.where(keep_tap, part, 0.0).astype(bf))
    moved = dot(jnp.concatenate(spread, 0), move)
    left = lax.broadcasted_iota(jnp.int32, (16, 128), 1) < STEP
    for g in range(10):
        for n in range(2):
            lanes = slice(128 * n, 128 * (n + 1))
            pair = jnp.where(left, moved[32 * g:32 * g + 16, lanes], moved[32 * g + 16:32 * g + 32, lanes]).astype(bf)
            for copy in range(3):
                p_ref[32 * copy + 16 * n:32 * copy + 16 * (n + 1), 128 * g:128 * (g + 1)] = pair

    def conv1(i, _):
        r = rows(i, M1)
        c_ref[r, :] = dot(p_ref[:, r], wc_ref[...], TN)
        return 0
    lax.fori_loop(0, total // M1, conv1, 0)

    def level_one(t, below):
        for j in reversed(range(TA // SA)):
            below = level_one_rows(pl.ds(pl.multiple_of(t * TA + j * SA, SA), SA), below)
        return below

    def level_one_rows(r, below):
        for half in range(2):
            c = c_ref[r, half * WIDTH:(half + 1) * WIDTH]
            inv = lax.rsqrt(lane_sum(c * c) * (1.0 / WIDTH) + 1e-5)
            y = c * inv * gain1 + shift1
            phi, e = gelu_parts(y)
            h = y * phi
            sg_ref[half, r, :] = (phi + (y * 0.3989422804014327) * e) * gain1
            r1_ref[half, r, :] = inv
            u_ref[r, half * WIDTH:(half + 1) * WIDTH] = h.astype(bf)
            if half == 0:
                u_ref[r, 2 * WIDTH:] = shifted_up(h, below).astype(bf)
                first = h[0:8]
        return first

    def conv2(t):
        r = rows(t, TA)
        s_ref[r, :] = dot(u_ref[r, :], w2_ref[...])

    def forward(i, below):
        t = total // TA - 2 - i
        conv2(t + 1)
        return level_one(t, below)
    below = level_one(total // TA - 1, zero)
    for load in loads[:8]:
        load.wait()
    lax.fori_loop(0, total // TA - 1, forward, below)
    conv2(0)

    loads[8].wait()

    def level_two(t, carry):
        for j in range(TB // SB):
            carry = level_two_rows(pl.multiple_of(t * TB + j * SB, SB), carry)
        return carry

    def level_two_rows(b, carry):
        acc_a, acc_b, above = carry
        r = pl.ds(b, SB)
        z = s_ref[r, :]
        c = z - lane_sum(z) * (1.0 / WIDTH)
        inv = lax.rsqrt(lane_sum(c * c) * (1.0 / WIDTH) + 1e-5)
        n = c * inv
        y = n * gain2 + shift2
        phi, e = gelu_parts(y)
        feat_ref[r, :] = (y * phi).astype(bf)
        slope = phi + (y * 0.3989422804014327) * e
        row = (lax.broadcasted_iota(jnp.int32, (SB, 1), 0) + b).astype(f32)
        room = jnp.where(row < ROWS, lengths[0], lengths[1] + 10.0 * ROWS)
        weight = jnp.where(10.0 * row + 19.0 < room, LOSS_SCALE, 0.0)
        q = cot_ref[r, :].astype(f32) * weight * (slope * gain2)
        back, qn = norm_back(q, n, inv)
        dl_ref[r, 0:WIDTH] = back.astype(bf)
        dl_ref[r, WIDTH:] = shifted_down(back, above).astype(bf)
        return acc_a + rows8(qn), acc_b + rows8(q), back[SB - 8:SB]

    def down(t):
        r = rows(t, TB)
        now = dl_ref[r, 0:WIDTH]
        d_ref[r, 0:WIDTH] = dot(now, w2_ref[0:WIDTH, :], NT) + dot(dl_ref[r, WIDTH:], w2_ref[2 * WIDTH:, :], NT)
        d_ref[r, WIDTH:] = dot(now, w2_ref[WIDTH:2 * WIDTH, :], NT)

    def middle(t, carry):
        down(t - 1)
        return level_two(t, carry)
    carry = level_two(0, (zero, zero, zero))
    acc_a, acc_b, _ = lax.fori_loop(1, total // TB, middle, carry)
    down(total // TB - 1)
    small_ref[12:13, :] = jnp.sum(acc_a, axis=0, keepdims=True) / gain2
    small_ref[13:14, :] = jnp.sum(acc_b, axis=0, keepdims=True) / gain2
    small_ref[14:16, :] = jnp.zeros((2, WIDTH), f32)

    def level_one_back(r, acc_a, acc_b):
        for half in range(2):
            lanes = slice(half * WIDTH, (half + 1) * WIDTH)
            q = d_ref[r, lanes] * sg_ref[half, r, :]
            inv = r1_ref[half, r, :]
            back, qn = norm_back(q, c_ref[r, lanes] * inv, inv)
            t_ref[r, lanes] = back.astype(bf)
            acc_a = acc_a + rows8(qn)
            acc_b = acc_b + rows8(q)
        return acc_a, acc_b

    def backward(i, acc):
        acc_a, acc_b = acc
        chunk = 3 * WIDTH // (total // TC)
        for ref, half in ((keep_ref, core), (send_ref, 1 - core)):
            cols = pl.ds(pl.multiple_of(half * HALF, HALF), HALF)
            grad = dot(u_ref[:, pl.ds(pl.multiple_of(i * chunk, chunk), chunk)], dl_ref[:, cols], TN).astype(ref.dtype)
            blocks = chunk // BLOCK
            for b in range(blocks):
                for j in range(4):
                    start = b * BLOCK + j * PART
                    ref[4 * j + blocks * i + b, 0:PART, :] = grad[start:start + PART]
        for j in range(TC // SC):
            acc_a, acc_b = level_one_back(pl.ds(pl.multiple_of(i * TC + j * SC, SC), SC), acc_a, acc_b)
        return acc_a, acc_b
    acc_a, acc_b = lax.fori_loop(0, total // TC, backward, (zero, zero))
    small_ref[10:11, :] = jnp.sum(acc_a, axis=0, keepdims=True) / gain1
    small_ref[11:12, :] = jnp.sum(acc_b, axis=0, keepdims=True) / gain1
    taps = dot(p_ref[0:32, :], t_ref[...])
    odd = jnp.concatenate([taps[5:10, WIDTH:], taps[16:21, WIDTH:]], 0)
    small_ref[0:10, :] = taps[0:10, 0:WIDTH] + odd
    small = small_ref[...].astype(bf)
    for j in range(4):
        quarter = jnp.concatenate([small[:, 128 * j:128 * (j + 1)], jnp.zeros((16, 128), bf)], 1)
        for i in range(4):
            send_ref[4 * j + i, PART:SLOTS, :] = quarter
            keep_ref[4 * j + i, PART:SLOTS, :] = quarter.astype(f32)


def encoder(ids, source, wc, par, own, other, cot, mine, theirs):
    total = cot.shape[0]
    vm = pl.BlockSpec(memory_space=pltpu.VMEM)
    hbm = pl.BlockSpec(memory_space=pl.ANY)
    return pl.pallas_call(
        encoder_kernel,
        out_shape=(
            jax.ShapeDtypeStruct((total, WIDTH), bf),
            jax.ShapeDtypeStruct((16, SLOTS, HALF), f32),
            jax.ShapeDtypeStruct((16, SLOTS, HALF), bf),
        ),
        in_specs=[pl.BlockSpec(memory_space=pltpu.SMEM)] * 2 + [vm] * 2 + [hbm] * 5,
        out_specs=(vm,) * 3,
        scratch_shapes=[
            pltpu.VMEM((2,) + own.shape[1:], bf),
            pltpu.SemaphoreType.DMA((2,)),
            pltpu.VMEM((3 * WIDTH, WIDTH), bf),
            pltpu.VMEM((total, WIDTH), bf),
            pltpu.SemaphoreType.DMA((9,)),
            pltpu.VMEM((96, total), bf),
            pltpu.VMEM((16, WIDTH), f32),
            pltpu.VMEM((total, 2 * WIDTH), f32),
            pltpu.VMEM((total, 3 * WIDTH), bf),
            pltpu.VMEM((total, WIDTH), f32),
            pltpu.VMEM((total, 2 * WIDTH), f32),
            pltpu.VMEM((2, total, WIDTH), f32),
            pltpu.VMEM((2, total, 1), f32),
            pltpu.VMEM((total, 2 * WIDTH), bf),
            pltpu.VMEM((total, 2 * WIDTH), bf),
        ],
        compiler_params=pltpu.CompilerParams(vmem_limit_bytes=VMEM_LIMIT),
        name="encoder",
    )(ids, source, wc, par, own, other, cot, mine, theirs)


def prep_weights(conv1_weight):
    w1 = conv1_weight.astype(f32)
    wc = w1 - jnp.mean(w1, axis=1, keepdims=True)
    even = jnp.pad(wc, ((0, 22), (0, 0)))
    odd = jnp.pad(jnp.concatenate([wc[:5], jnp.zeros((6, WIDTH), f32), wc[5:]], 0), ((5, 11), (0, 0)))
    both = jnp.concatenate([even, odd], 1)
    hi = lax.reduce_precision(both, 8, 7)
    mid = lax.reduce_precision(both - hi, 8, 7)
    low = both - hi - mid
    return jnp.concatenate([hi.astype(bf), mid.astype(bf), low.astype(bf)], 0)


def pack_kernel(lengths_ref, wave_ref, out_ref):
    row = lax.broadcasted_iota(jnp.int32, (2, SAMPLES), 0)
    at = lax.broadcasted_iota(jnp.int32, (2, SAMPLES), 1)
    end = jnp.where(row == 0, lengths_ref[0], lengths_ref[1])
    cleaned = jnp.where(at < end, wave_ref[...].astype(f32), 0.0)
    lane, last = at[:, :128], end[:, :128]
    code = jnp.where(lane == 0, last >> 7, jnp.where(lane == 1, last & 127, 0)).astype(f32)
    block = jnp.concatenate([cleaned, code], 1).astype(bf)
    for k in range(out_ref.shape[0]):
        out_ref[k] = block


def pack(waveform, lengths, copies):
    return pl.pallas_call(
        pack_kernel,
        out_shape=jax.ShapeDtypeStruct((copies, 2, SAMPLES + 128), bf),
        in_specs=[pl.BlockSpec(memory_space=pltpu.SMEM), pl.BlockSpec(memory_space=pltpu.VMEM)],
        out_specs=pl.BlockSpec(memory_space=pltpu.VMEM),
        name="pack",
    )(lengths, waveform)


Y, Z, C, X = 4, 8, 2, 4
AXES = ("y", "z", "c", "x")


def flip(value, axis, size, k):
    return lax.ppermute(value, axis, [(i, i ^ k) for i in range(size)])


def turn(value, axis, size, k):
    return lax.ppermute(value, axis, [(i, (i + k) % size) for i in range(size)])


def exchange(chunks, axes):
    return lax.all_to_all(chunks, axes, 0, 0, tiled=True)


def reduce_grads(keep, send, core, shadow):
    chunks = (keep + flip(send, "c", C, 1).astype(f32)).astype(bf)
    total = jnp.sum(exchange(chunks, ("y", "x")).astype(f32), axis=0).astype(bf)
    total, shadow = lax.optimization_barrier((total, shadow))
    a, b, c = (turn(total, "z", Z, k).astype(f32) for k in (2, 4, 6))
    total = ((total.astype(f32) + b) + (a + c)).astype(bf)
    total = (total.astype(f32) + flip(total, "z", Z, 1).astype(f32)).astype(bf)
    quarters = jnp.stack([total] + [flip(total, "y", Y, k) for k in (1, 2, 3)])
    y = lax.axis_index("y")
    every = jnp.concatenate([lax.dynamic_slice_in_dim(quarters, y ^ q, 1, 0) for q in range(Y)], 0)
    half = every[:, :PART].reshape(-1, HALF)
    other = flip(half, "c", C, 1)
    grad_conv2 = jnp.where(core == 0, jnp.concatenate([half, other], 1), jnp.concatenate([other, half], 1))
    small = jnp.concatenate([every[q, PART:PART + 14, :128] for q in range(Y)], 1)
    return grad_conv2.astype(f32), small.astype(f32), shadow


def body(waveform, lengths, source, frame_mask, cotangent, conv1_weight, gain_one, shift_one,
         conv2_weight, gain_two, shift_two):
    count, frames = frame_mask.shape
    core, x = lax.axis_index("c"), lax.axis_index("x")
    column = exchange(pack(waveform, lengths, Y * Z), ("y", "z"))
    strip = lax.dynamic_slice_in_dim(conv2_weight, core * STRIP, STRIP, 0)
    pair = jnp.concatenate([strip, flip(strip, "x", X, 1)], 0)
    mine = jnp.concatenate([pair, flip(pair, "x", X, 2)], 0)
    theirs = flip(mine, "c", C, 1)
    masked = cotangent * frame_mask[:, :, None].astype(bf)
    upstream = jnp.pad(masked, ((0, 0), (0, 1), (0, 0))).reshape(count * ROWS, WIDTH)
    par = jnp.concatenate(
        [jnp.stack([gain_one, shift_one, gain_two, shift_two]), jnp.zeros((4, WIDTH), f32)], 0)
    wc = prep_weights(conv1_weight)
    ids = jnp.stack([core, x])
    column, mine, theirs, upstream, par, wc, ids = lax.optimization_barrier(
        (column, mine, theirs, upstream, par, wc, ids))
    feat, keep, send = encoder(ids, source, wc, par, column, flip(column, "c", C, 1), upstream, mine, theirs)
    features = feat.reshape(count, ROWS, WIDTH)[:, :frames]
    grad_conv2, grad_front, features = reduce_grads(keep, send, core, features)
    return features, grad_conv2, grad_front


def solution(mesh):
    grid = Mesh(mesh.devices.reshape(Y, Z, C, X), AXES)
    both = P(AXES)
    placed = (both, both, both, both, both, P(), P(), P(), P("x"), P(), P())
    return jax.shard_map(
        body,
        mesh=grid,
        in_specs=placed,
        out_specs=(both, P("x"), P()),
        check_vma=False,
    )
```
